128 devices in a mesh: tile: 32 (over z, y, core), rep: 4 (over x).
Axes of the slice: x: 4, y: 4, z: 4, core: 2. Of those that a mesh axis runs over, the one named last changes fastest.
Arguments:
- amplitudes: bfloat16 [1024, 32, 1024], P('tile'), may hold values from -6 to 6
- integrals: bfloat16 [32, 16, 1024, 1024], P('tile', 'rep'), may hold values from -0.09375 to 0.09375
- owner_order: int32 [32], replicated, may hold values from 0 to 31, each once
- screen_list: int32 [32, 16], replicated, may hold values from 0 to 31, as said below
- live_mask: int32 [32, 16], replicated, may hold values 0 or 1
Outputs:
- ladder: float32 [1024, 32, 1024], P('tile', 'rep')
The draws below stay inside these ranges and needn't reach their ends.
Inputs may be any that keep to these rules, and one draw needn't show every extreme that they name: `screen_list`: slot s of every row names a tile of block s mod 4, block q holding tiles q * 8 to (q + 1) * 8 - 1.
All inputs are finite; a program needn't handle non-finite values.
Results may differ from the reference program's by a relative error of at most 0.0029.
Values may be sent and summed in bfloat16 or wider, within the bound.
A program may use at most 128 MiB of HBM per device.

```python
import jax
import jax.numpy as jnp
from jax import lax

PW = 1024
KS_DEV = 4
NPT = 32
KS = 16
MROWS = 1024
N_REP = 4


def draw_screen_list(key, part):
    key = jax.random.fold_in(key, 5)
    block_width = NPT // N_REP
    slot_ids = jnp.arange(KS, dtype=jnp.int32)
    block_ids = slot_ids % KS_DEV // (KS_DEV // N_REP)
    offset = jax.random.randint(key, (NPT, KS), 0, block_width, dtype=jnp.int32)
    offset = offset.at[0, 0].set(0).at[0, KS - 1].set(block_width - 1)
    return (block_ids[None, :] * block_width + offset).astype(jnp.int32)


def with_ends(values, own_key, low, largest):
    longest = values.shape.index(max(values.shape))
    spots = []
    for shift in (0, 1):
        where = [jax.random.randint(jax.random.fold_in(own_key, axis), (), 0, length) for axis, length in enumerate(values.shape)]
        where[longest] = (where[longest] + shift) % values.shape[longest]
        spots.append(tuple(where))
    return values.at[spots[0]].set(low).at[spots[1]].set(largest)


def block_levels(key, extent, cuts, low, high):
    loudness, own = 1.0, jax.random.fold_in(key, 6)
    for dim, shards_of in cuts:
        steps = jnp.exp(jax.random.uniform(jax.random.fold_in(own, dim), (shards_of,), jnp.float32, low / len(cuts), high / len(cuts)))
        loudness = loudness * jnp.repeat(steps, extent[dim] // shards_of).reshape([-1 if axis == dim else 1 for axis in range(len(extent))])
    return loudness


def normal_values(stream_key, extent, scale, bound, shards=(), kind=jnp.bfloat16):
    factor_of = block_levels(stream_key, extent, shards, -0.22, 0.18) if shards else 1.0
    entries = jax.random.normal(stream_key, extent, jnp.float32) * scale * factor_of
    return jnp.minimum(jnp.maximum(entries, -bound), bound).astype(kind)


def setup_inputs(seed: int = 0) -> dict:
    splits = jax.random.split(jax.random.key(seed), 6)
    return {
        "amplitudes": normal_values(splits[0], (MROWS, NPT, PW), 1.0, 6.0, ((0, 32),)),
        "integrals": normal_values(splits[1], (NPT, KS, PW, PW), (4 * PW) ** -0.5, 0.09375, ((0, 32), (1, 4))),
        "owner_order": jax.random.permutation(splits[2], NPT).astype(jnp.int32),
        "screen_list": draw_screen_list(jax.random.fold_in(splits[5], 71), 0),
        "live_mask": with_ends((jax.random.randint(splits[4], (NPT, KS), 0, 4) < 3).astype(jnp.int32), jax.random.fold_in(splits[4], 1), 0, 1),
    }


def reference(amplitudes, integrals, owner_order, screen_list, live_mask):
    ordered = jnp.take(amplitudes, owner_order, axis=1)
    tile_ids = jnp.arange(NPT, dtype=jnp.int32)

    def add_tile(accumulated, position):
        column = lax.dynamic_index_in_dim(ordered, position, 1, keepdims=False).astype(jnp.float32)
        block = lax.dynamic_index_in_dim(integrals, position, 0, keepdims=False).astype(jnp.float32)
        live_row = lax.dynamic_index_in_dim(live_mask, position, 0, keepdims=False).astype(jnp.float32)
        labels = lax.dynamic_index_in_dim(screen_list, position, 0, keepdims=False)
        pieces = jnp.einsum("mc,scd->msd", column, block)
        pieces = (pieces * live_row[None, :, None]).astype(jnp.bfloat16)
        pieces = lax.optimization_barrier(pieces).astype(jnp.float32)
        onehot = (labels[:, None] == tile_ids[None, :]).astype(jnp.float32)
        return accumulated + jnp.einsum("msd,sa->mad", pieces, onehot), None

    start = jnp.zeros((MROWS, NPT, PW), jnp.float32)
    ladder, unused = lax.scan(add_tile, start, jnp.arange(NPT, dtype=jnp.int32))
    return ladder
```

```python
import functools

import jax
import jax.numpy as jnp
from jax import lax
from jax.experimental import pallas as pl
from jax.experimental.pallas import tpu as pltpu
from jax.sharding import PartitionSpec as P

MESH = pl.DeviceIdType.MESH
BF16, F32, I32 = jnp.bfloat16, jnp.float32, jnp.int32
NAT = ("x1", "x0", "z1", "z0", "y1", "y0")
ORDER = ("x0", "y0", "z0", "x1", "y1", "z1")
STREAMS = ((0, 0, 384), (0, 384, 384), (0, 768, 256), (1, 0, 384), (1, 384, 384), (1, 768, 256))


def bits_of(r):
    return [ORDER[(r + i) % 6] for i in range(6)]


def last_z(r):
    return [b for b in bits_of(r) if b[0] == "z"][1]


def gray(v):
    return v + v // 2 - 2 * (v // 3)


def left(r, used):
    gone = bits_of(r)[:used]
    return [b for b in NAT if b not in gone]


def view(ref, lead, names, fixed, tail=()):
    return ref.at[tuple(lead) + tuple(fixed[b] if b in fixed else slice(None) for b in names) + tuple(tail)]


def kernel(owner, screen, live, amp_hbm, int_hbm, out, amp, ints, ordered, column, pieces, weights, *rest):
    r1, r2, r3, s4, r4, k4, s5, r5, k5, s6, r6 = (rest[6 * i : 6 * i + 6] for i in range(11))
    load_sem, amp_sem, send_sem, sem1, sem2, sem3, sem4, sem5, sem6 = rest[66:]
    x, t = lax.axis_index("rep"), lax.axis_index("tile")
    z, y, c = t // 8, (t // 2) % 4, t % 2
    g = {"x": gray(x), "y": gray(y), "z": gray(z)}
    mine = {a + "1": g[a] // 2 for a in g} | {a + "0": g[a] % 2 for a in g}
    other = {b: 1 - mine[b] for b in mine}

    def device(flips, core):
        at = {a: gray((other if a + "1" in flips else mine)[a + "1"] * 2 + (other if a + "0" in flips else mine)[a + "0"]) for a in g}
        return (at["z"] * 8 + at["y"] * 2 + core, at["x"])

    sent = []

    def send(src, dst, sem, to):
        copy = pltpu.make_async_remote_copy(src, dst, send_sem, sem, device_id=to, device_id_type=MESH)
        copy.start()
        sent.append(copy)

    def wait(ref, sem):
        pltpu.make_async_copy(ref, ref, sem).wait()

    load_amp = pltpu.make_async_copy(amp_hbm, amp, load_sem.at[0])
    load_amp.start()
    load_ints = [pltpu.make_async_copy(int_hbm.at[j], ints.at[j], load_sem.at[1 + j]) for j in range(4)]
    for load in load_ints:
        load.start()

    barrier = pltpu.get_barrier_semaphore()

    @pl.loop(1, 32)
    def _(k):
        to = ((z + k // 8) % 4) * 8 + ((y + (k // 2) % 4) % 4) * 2 + (c + k) % 2
        pl.semaphore_signal(barrier, inc=1, device_id=(to, x), device_id_type=MESH)

    for b in ("x0", "x1"):
        for core in range(2):
            pl.semaphore_signal(barrier, inc=1, device_id=device((b,), core), device_id_type=MESH)

    lane = lax.broadcasted_iota(I32, (8, 256), 1)
    bin_of_row = lax.broadcasted_iota(I32, (8, 256), 0)
    for r in range(6):
        e = bits_of(r)
        x_left = [b for b in e[3:] if b[0] == "x"][0]
        for f in range(2):
            want = dict(mine)
            if f:
                want[x_left] = other[x_left]
            block = gray(want["x1"] * 2 + want["x0"])
            label = jnp.full((8, 256), -1, I32)
            for s in range(16):
                flips = [e[2 - i] for i in range(3) if (s >> (3 - i)) & 1]
                tile, rep = device(flips, s & 1)
                slot = rep * 4 + block
                found = jnp.where(live[tile, slot] != 0, screen[tile, slot] - 8 * block, -1)
                label = jnp.where(lane // 16 == s, found, label)
            hit = label == bin_of_row
            rows = [jnp.where(hit & (lane % 16 == m), 1.0, 0.0).astype(F32) for m in range(16)]
            weights[2 * r + f] = jnp.concatenate(rows, axis=0).astype(BF16)

    load_amp.wait()
    away = lax.broadcasted_iota(I32, (32, 1024), 1) - 32 * lax.broadcasted_iota(I32, (32, 1024), 0)

    @pl.loop(0, 4)
    def _(zz):
        pick = [jnp.where(away == owner[zz * 8 + i], 1.0, 0.0).astype(BF16) for i in range(8)]
        pick = jnp.concatenate(pick, axis=0)
        for n in range(2):
            got = jnp.dot(pick, amp[:, n * 512 : n * 512 + 512], preferred_element_type=F32)
            ordered[pl.ds(zz * 8, 8), :, n * 512 : n * 512 + 512] = got.astype(BF16).reshape(8, 32, 512)

    pl.semaphore_wait(barrier, 35)

    own_row = g["y"] * 2 + c
    own = pltpu.make_async_copy(ordered.at[t], column.at[g["z"], own_row], amp_sem.at[g["z"]])
    own.start()

    def amp_copy(dz, dy, dc):
        to = ((z + dz) % 4) * 8 + ((y + dy) % 4) * 2 + (c + dc) % 2
        send(ordered.at[to], column.at[g["z"], own_row], amp_sem.at[g["z"]], (to, x))

    for dz in (0, 1, 3, 2):
        for dy in (0, 1, 3, 2):
            for dc in (0, 1):
                if (dz, dy, dc) != (0, 0, 0):
                    amp_copy(dz, dy, dc)

    for load in load_ints:
        load.wait()

    slot_of = (0, 1, 3, 2)
    for k in range(4):
        zv = {"z1": (other if k >> 1 else mine)["z1"], "z0": (other if k & 1 else mine)["z0"]}
        gz = zv["z1"] * 2 + zv["z0"]
        wait(column.at[gz], amp_sem.at[gz])

        @pl.loop(0, 8)
        def _(step):
            j, cols = step // 2, pl.ds(pl.multiple_of((step % 2) * 512, 512), 512)
            left_side = column[gz].reshape(256, 1024)
            got = jnp.dot(left_side, ints[j, :, cols], preferred_element_type=F32).astype(BF16)
            gj = gray(j)
            pieces[gj // 2, gj % 2, zv["z1"], zv["z0"], :, :, :, :, :, cols] = got.reshape(2, 2, 2, 2, 16, 512)

        for r, (h, start, width) in enumerate(STREAMS):
            e1, zl = bits_of(r)[0], last_z(r)
            v = k >> 1 if zl == "z1" else k & 1
            sem = sem1.at[r, v]
            cols = pl.ds(start, width)
            flip_z = {"z0": k & 1, "z1": k >> 1}
            names = left(r, 1)

            def part(e1_value, core):
                return view(pieces, (), NAT, {e1: e1_value} | zv, (core, h, slice(None), cols))

            def place(a):
                return view(r1[r], (a, c), names, {b: n for b, n in zv.items() if b != e1})

            if e1[0] != "z" or flip_z[e1]:
                for core in range(2):
                    send(part(other[e1], core), place(1), sem, device((e1,), core))
            if e1[0] != "z" or not flip_z[e1]:
                send(part(mine[e1], 1 - c), place(0), sem, device((), 1 - c))
                pltpu.make_async_copy(part(mine[e1], c), place(0), sem).start()

    def zfix(r, v):
        zl = last_z(r)
        return {zl: (other if v else mine)[zl]}

    for v in range(2):
        for r in range(6):
            e1, e2, e3 = bits_of(r)[:3]
            fix = zfix(r, v)
            wait(view(r1[r], (slice(None), slice(None)), left(r, 1), fix), sem1.at[r, v])
            send(
                view(r1[r], (slice(None), slice(None)), left(r, 1), {e2: other[e2]} | fix),
                view(r2[r], (slice(None), slice(None)), left(r, 2), fix),
                sem2.at[r, v],
                device((e2,), c),
            )
            send(
                view(r1[r], (slice(None), slice(None)), left(r, 1), {e2: mine[e2], e3: other[e3]} | fix),
                view(r3[r], (0, slice(None), slice(None)), left(r, 3), fix),
                sem3.at[r, v],
                device((e3,), c),
            )
    for v in range(2):
        for r in range(6):
            e1, e2, e3 = bits_of(r)[:3]
            fix = zfix(r, v)
            wait(view(r2[r], (slice(None), slice(None)), left(r, 2), fix), sem2.at[r, v])
            send(
                view(r2[r], (slice(None), slice(None)), left(r, 2), {e3: other[e3]} | fix),
                view(r3[r], (1, slice(None), slice(None)), left(r, 3), fix),
                sem3.at[r, v],
                device((e3,), c),
            )

    def zlast_at(r):
        return bits_of(r).index(last_z(r)) - 3

    for v in range(2):
        for r in range(6):
            e = bits_of(r)
            fix = zfix(r, v)
            wait(view(r3[r], (slice(None),) * 3, left(r, 3), fix), sem3.at[r, v])
            at = zlast_at(r)
            for code in range(8):
                f = (code >> 2, (code >> 1) & 1, code & 1)
                if f[at] != v:
                    continue
                here = {b: (other if n else mine)[b] for b, n in zip(e[3:], f)}
                all_here = here | {e[1]: mine[e[1]], e[2]: mine[e[2]]}
                blocks = []
                for a in range(2):
                    for core in range(2):
                        blocks.append(r1[r][(a, core) + tuple(all_here[b] for b in left(r, 1))])
                for a in range(2):
                    for core in range(2):
                        blocks.append(r2[r][(a, core) + tuple(all_here[b] for b in left(r, 2))])
                for b2 in range(2):
                    for a in range(2):
                        for core in range(2):
                            blocks.append(r3[r][(b2, a, core) + tuple(all_here[b] for b in left(r, 3))])
                x_at = [b[0] for b in e[3:]].index("x")
                binned = jnp.dot(weights[2 * r + f[x_at]], jnp.concatenate(blocks, axis=0), preferred_element_type=F32)
                if f[0]:
                    s4[r][f[1], f[2]] = binned.astype(BF16)
                else:
                    k4[r][f[1], f[2]] = binned
            to = device((e[3],), c)
            if at == 2:
                send(s4[r].at[:, v], r4[r].at[:, v], sem4.at[r, v], to)
            elif at == 1:
                send(s4[r].at[v], r4[r].at[v], sem4.at[r, v], to)
            elif v == 1:
                send(s4[r], r4[r], sem4.at[r, 0], to)

    def step5(r, f5, f6):
        total = k4[r][f5, f6] + r4[r][f5, f6].astype(F32)
        if f5:
            s5[r][f6] = total.astype(BF16)
        else:
            k5[r][f6] = total

    for v in range(2):
        for r in range(6):
            at = zlast_at(r)
            to = device((bits_of(r)[4],), c)
            if at == 2:
                wait(r4[r].at[:, v], sem4.at[r, v])
                step5(r, 1, v)
                send(s5[r].at[v], r5[r].at[v], sem5.at[r, v], to)
                step5(r, 0, v)
            elif at == 1:
                u = 1 - v
                wait(r4[r].at[u], sem4.at[r, u])
                step5(r, u, 0)
                step5(r, u, 1)
                if u:
                    send(s5[r], r5[r], sem5.at[r, 0], to)
            elif v == 1:
                wait(r4[r], sem4.at[r, 0])
                step5(r, 1, 0)
                step5(r, 1, 1)
                send(s5[r], r5[r], sem5.at[r, 0], to)
                step5(r, 0, 0)
                step5(r, 0, 1)

    for r in range(6):
        if zlast_at(r) == 2:
            wait(r5[r].at[1], sem5.at[r, 1])
        else:
            wait(r5[r], sem5.at[r, 0])
        s6[r][...] = (k5[r][1] + r5[r][1].astype(F32)).astype(BF16)
        send(s6[r], r6[r], sem6.at[r], device((bits_of(r)[5],), c))
    for r, (h, start, width) in enumerate(STREAMS):
        if zlast_at(r) == 2:
            wait(r5[r].at[0], sem5.at[r, 0])
        wait(r6[r], sem6.at[r])
        total = k5[r][0] + r5[r][0].astype(F32) + r6[r][...].astype(F32)
        out[16 * h : 16 * h + 16, :, start : start + width] = total.reshape(16, 8, width)

    for copy in sent:
        copy.wait_send()


def on_device(amplitudes, integrals, owner_order, screen_list, live_mask):
    rows, tiles, width = amplitudes.shape
    widths = [w for _, _, w in STREAMS]

    def group(lead, tail, dtype):
        return [pltpu.VMEM(lead + tail(w), dtype) for w in widths]

    two = (2,)
    raw = lambda w: (16, w)
    dense = lambda w: (128, w)
    scratch = [
        pltpu.VMEM((rows * tiles, width), BF16),
        pltpu.VMEM((4, width, width), BF16),
        pltpu.VMEM((tiles, rows, width), BF16),
        pltpu.VMEM((4, 8, rows, width), BF16),
        pltpu.VMEM(two * 8 + (16, width), BF16),
        pltpu.VMEM((12, 128, 256), BF16),
        *group(two * 7, raw, BF16),
        *group(two * 6, raw, BF16),
        *group(two * 6, raw, BF16),
        *group(two * 2, dense, BF16),
        *group(two * 2, dense, BF16),
        *group(two * 2, dense, F32),
        *group(two, dense, BF16),
        *group(two, dense, BF16),
        *group(two, dense, F32),
        *group((), dense, BF16),
        *group((), dense, BF16),
        pltpu.SemaphoreType.DMA((5,)),
        pltpu.SemaphoreType.DMA((4,)),
        pltpu.SemaphoreType.DMA,
        *[pltpu.SemaphoreType.DMA((6, 2))] * 5,
        pltpu.SemaphoreType.DMA((6,)),
    ]
    smem = pl.BlockSpec(memory_space=pltpu.SMEM)
    hbm = pl.BlockSpec(memory_space=pl.ANY)
    return pl.pallas_call(
        kernel,
        out_shape=jax.ShapeDtypeStruct((rows, 8, width), F32),
        in_specs=[smem, smem, smem, hbm, hbm],
        out_specs=pl.BlockSpec(memory_space=pltpu.VMEM),
        scratch_shapes=scratch,
        cost_estimate=pl.CostEstimate(flops=13_000_000_000, bytes_accessed=12 << 20, transcendentals=0),
        compiler_params=pltpu.CompilerParams(
            collective_id=0, has_side_effects=True, vmem_limit_bytes=60 << 20
        ),
    )(owner_order, screen_list, live_mask, amplitudes.reshape(rows * tiles, width), integrals[0])


def solution(mesh):
    in_specs = (P("tile", None, None), P("tile", "rep", None, None), P(), P(), P())
    out_specs = P("tile", "rep", None)
    return jax.shard_map(
        on_device, mesh=mesh, in_specs=in_specs, out_specs=out_specs, check_vma=False
    )
```

```python
import functools

import jax
import jax.numpy as jnp
from jax import lax
from jax.experimental import pallas as pl
from jax.experimental.pallas import tpu as pltpu
from jax.sharding import PartitionSpec as P

MESH = pl.DeviceIdType.MESH
BF16, F32, I32 = jnp.bfloat16, jnp.float32, jnp.int32
NAT = ("x1", "x0", "z1", "z0", "y1", "y0")
ORDER = ("x0", "y0", "z0", "x1", "y1", "z1")
STREAMS = ((0, 0, 384), (0, 384, 384), (0, 768, 256), (1, 0, 384), (1, 384, 384), (1, 768, 256))
CHUNKS, HALVES = (1, 2, 3, 0), (1, 0)


def bits_of(r):
    return [ORDER[(r + i) % 6] for i in range(6)]


def last_z(r):
    return [b for b in bits_of(r) if b[0] == "z"][1]


def gray(v):
    return v + v // 2 - 2 * (v // 3)


def left(r, used):
    gone = bits_of(r)[:used]
    return [b for b in NAT if b not in gone]


def view(ref, lead, names, fixed, tail=()):
    return ref.at[tuple(lead) + tuple(fixed[b] if b in fixed else slice(None) for b in names) + tuple(tail)]


def kernel(owner, screen, live, amp_hbm, int_hbm, out, amp, ints, ordered, column, pieces, weights, *rest):
    r1, r2, r3, s4, r4, k4, s5, r5, k5, s6, r6 = (rest[6 * i : 6 * i + 6] for i in range(11))
    load_sem, amp_sem, far_sem, send_sem, sem1, sem2, sem3, sem4, sem5, sem6 = rest[66:]
    x, t = lax.axis_index("rep"), lax.axis_index("tile")
    z, y, c = t // 8, (t // 2) % 4, t % 2
    g = {"x": gray(x), "y": gray(y), "z": gray(z)}
    mine = {a + "1": g[a] // 2 for a in g} | {a + "0": g[a] % 2 for a in g}
    other = {b: 1 - mine[b] for b in mine}

    def device(flips, core):
        at = {a: gray((other if a + "1" in flips else mine)[a + "1"] * 2 + (other if a + "0" in flips else mine)[a + "0"]) for a in g}
        return (at["z"] * 8 + at["y"] * 2 + core, at["x"])

    sent = []

    def send(src, dst, sem, to):
        copy = pltpu.make_async_remote_copy(src, dst, send_sem, sem, device_id=to, device_id_type=MESH)
        copy.start()
        sent.append(copy)

    def wait(ref, sem):
        pltpu.make_async_copy(ref, ref, sem).wait()

    load_amp = pltpu.make_async_copy(amp_hbm, amp, load_sem.at[0])
    load_amp.start()
    load_ints = [pltpu.make_async_copy(int_hbm.at[j], ints.at[j], load_sem.at[1 + j]) for j in range(4)]

    barrier = pltpu.get_barrier_semaphore()

    @pl.loop(1, 32)
    def _(k):
        to = ((z + k // 8) % 4) * 8 + ((y + (k // 2) % 4) % 4) * 2 + (c + k) % 2
        pl.semaphore_signal(barrier, inc=1, device_id=(to, x), device_id_type=MESH)

    for b in ("x0", "x1"):
        for core in range(2):
            pl.semaphore_signal(barrier, inc=1, device_id=device((b,), core), device_id_type=MESH)
    pl.semaphore_signal(barrier, inc=1, device_id=device(("x0", "x1"), c), device_id_type=MESH)

    def far(n):
        return ((2, x // 2), (2, 2 + x // 2), (1, 2 - x // 2), (3, 2 + x // 2))[n] + (x % 2,)

    load_amp.wait()
    for load in load_ints:
        load.start()
    away = lax.broadcasted_iota(I32, (32, 1024), 1) - 32 * lax.broadcasted_iota(I32, (32, 1024), 0)
    own_row = g["y"] * 2 + c
    near = [(dz, dy, dc) for dz, dy in ((1, 0), (1, 3), (3, 0), (3, 1), (0, 1), (0, 3), (0, 0), (0, 2)) for dc in (0, 1)]
    blocks = [far(n) for n in (2, 3, 0, 1)] + near
    for first in (0, 8, 16):
        some = blocks[first : first + 8]
        to = [((z + dz) % 4) * 8 + ((y + dy) % 4) * 2 + (c + dc) % 2 for dz, dy, dc in some]
        pick = [jnp.where(away == owner[p], 1.0, 0.0).astype(BF16) for p in to]
        pick = jnp.concatenate(pick, axis=0)
        for n in range(2):
            got = jnp.dot(pick, amp[:, n * 512 : n * 512 + 512], preferred_element_type=F32)
            ordered[first : first + len(some), :, n * 512 : n * 512 + 512] = got.astype(BF16).reshape(len(some), 32, 512)
        if first == 0:
            pl.semaphore_wait(barrier, 36)
        for i, p in enumerate(to):
            src, dst = ordered.at[first + i], column.at[g["z"], own_row]
            if some[i] == (0, 0, 0):
                pltpu.make_async_copy(src, dst, amp_sem.at[g["z"]]).start()
            elif first == 0 and i < 4:
                send(src, dst, far_sem.at[(2, 3, 0, 1)[i]], (p, x))
            else:
                send(src, dst, amp_sem.at[g["z"]], (p, x))

    lane = lax.broadcasted_iota(I32, (8, 256), 1)
    bin_of_row = lax.broadcasted_iota(I32, (8, 256), 0)
    for r in range(6):
        e = bits_of(r)
        x_left = [b for b in e[3:] if b[0] == "x"][0]
        for f in range(2):
            want = dict(mine)
            if f:
                want[x_left] = other[x_left]
            block = gray(want["x1"] * 2 + want["x0"])
            label = jnp.full((8, 256), -1, I32)
            for s in range(16):
                flips = [e[2 - i] for i in range(3) if (s >> (3 - i)) & 1]
                tile, rep = device(flips, s & 1)
                slot = rep * 4 + block
                found = jnp.where(live[slot, tile] != 0, screen[slot, tile] - 8 * block, -1)
                label = jnp.where(lane // 16 == s, found, label)
            hit = label == bin_of_row
            rows = [jnp.where(hit & (lane % 16 == m), 1.0, 0.0).astype(F32) for m in range(16)]
            weights[2 * r + f] = jnp.concatenate(rows, axis=0).astype(BF16)

    for n in (2, 3, 0, 1):
        dz, dy, dc = far(n)
        gz = gray((z - dz + 4) % 4)
        block = column.at[gz, gray((y - dy + 4) % 4) * 2 + (c + dc) % 2]
        wait(block, far_sem.at[n])
        for dx in (1, 3, 2):
            send(block, block, amp_sem.at[gz], (t, (x + dx) % 4))

    for load in load_ints:
        load.wait()

    for k in CHUNKS:
        zv = {"z1": (other if k >> 1 else mine)["z1"], "z0": (other if k & 1 else mine)["z0"]}
        gz = zv["z1"] * 2 + zv["z0"]
        wait(column.at[gz, pl.ds(0, (8, 7, 7, 6)[k])], amp_sem.at[gz])

        @pl.loop(0, 4)
        def _(j):
            left_side = column[gz].reshape(256, 1024)
            got = jnp.dot(left_side, ints[j], preferred_element_type=F32).astype(BF16)
            gj = gray(j)
            pieces[gj // 2, gj % 2, zv["z1"], zv["z0"]] = got.reshape(2, 2, 2, 2, 16, 1024)

        for r, (h, start, width) in enumerate(STREAMS):
            e1, zl = bits_of(r)[0], last_z(r)
            v = k >> 1 if zl == "z1" else k & 1
            sem = sem1.at[r, v]
            cols = pl.ds(start, width)
            flip_z = {"z0": k & 1, "z1": k >> 1}
            names = left(r, 1)

            def part(e1_value, core):
                return view(pieces, (), NAT, {e1: e1_value} | zv, (core, h, slice(None), cols))

            def place(a):
                return view(r1[r], (a, c), names, {b: n for b, n in zv.items() if b != e1})

            if e1[0] != "z" or flip_z[e1]:
                for core in range(2):
                    send(part(other[e1], core), place(1), sem, device((e1,), core))
            if e1[0] != "z" or not flip_z[e1]:
                send(part(mine[e1], 1 - c), place(0), sem, device((), 1 - c))
                pltpu.make_async_copy(part(mine[e1], c), place(0), sem).start()

    def zfix(r, v):
        zl = last_z(r)
        return {zl: (other if v else mine)[zl]}

    for v in HALVES:
        for r in range(6):
            e1, e2, e3 = bits_of(r)[:3]
            fix = zfix(r, v)
            wait(view(r1[r], (slice(None), slice(None)), left(r, 1), fix), sem1.at[r, v])
            send(
                view(r1[r], (slice(None), slice(None)), left(r, 1), {e2: other[e2]} | fix),
                view(r2[r], (slice(None), slice(None)), left(r, 2), fix),
                sem2.at[r, v],
                device((e2,), c),
            )
            send(
                view(r1[r], (slice(None), slice(None)), left(r, 1), {e2: mine[e2], e3: other[e3]} | fix),
                view(r3[r], (0, slice(None), slice(None)), left(r, 3), fix),
                sem3.at[r, v],
                device((e3,), c),
            )
    for v in HALVES:
        for r in range(6):
            e1, e2, e3 = bits_of(r)[:3]
            fix = zfix(r, v)
            wait(view(r2[r], (slice(None), slice(None)), left(r, 2), fix), sem2.at[r, v])
            send(
                view(r2[r], (slice(None), slice(None)), left(r, 2), {e3: other[e3]} | fix),
                view(r3[r], (1, slice(None), slice(None)), left(r, 3), fix),
                sem3.at[r, v],
                device((e3,), c),
            )

    def zlast_at(r):
        return bits_of(r).index(last_z(r)) - 3

    for v in HALVES:
        for r in range(6):
            e = bits_of(r)
            fix = zfix(r, v)
            wait(view(r3[r], (slice(None),) * 3, left(r, 3), fix), sem3.at[r, v])
            at = zlast_at(r)
            for code in range(8):
                f = (code >> 2, (code >> 1) & 1, code & 1)
                if f[at] != v:
                    continue
                here = {b: (other if n else mine)[b] for b, n in zip(e[3:], f)}
                all_here = here | {e[1]: mine[e[1]], e[2]: mine[e[2]]}
                blocks = []
                for a in range(2):
                    for core in range(2):
                        blocks.append(r1[r][(a, core) + tuple(all_here[b] for b in left(r, 1))])
                for a in range(2):
                    for core in range(2):
                        blocks.append(r2[r][(a, core) + tuple(all_here[b] for b in left(r, 2))])
                for b2 in range(2):
                    for a in range(2):
                        for core in range(2):
                            blocks.append(r3[r][(b2, a, core) + tuple(all_here[b] for b in left(r, 3))])
                x_at = [b[0] for b in e[3:]].index("x")
                binned = jnp.dot(weights[2 * r + f[x_at]], jnp.concatenate(blocks, axis=0), preferred_element_type=F32)
                if f[0]:
                    s4[r][f[1], f[2]] = binned.astype(BF16)
                else:
                    k4[r][f[1], f[2]] = binned
            to = device((e[3],), c)
            if at == 2:
                send(s4[r].at[:, v], r4[r].at[:, v], sem4.at[r, v], to)
            elif at == 1:
                send(s4[r].at[v], r4[r].at[v], sem4.at[r, v], to)
            elif v == 1:
                send(s4[r], r4[r], sem4.at[r, 0], to)

    def step5(r, f5, f6):
        total = k4[r][f5, f6] + r4[r][f5, f6].astype(F32)
        if f5:
            s5[r][f6] = total.astype(BF16)
        else:
            k5[r][f6] = total

    for v in HALVES:
        for r in range(6):
            at = zlast_at(r)
            to = device((bits_of(r)[4],), c)
            if at == 2:
                wait(r4[r].at[:, v], sem4.at[r, v])
                step5(r, 1, v)
                send(s5[r].at[v], r5[r].at[v], sem5.at[r, v], to)
                step5(r, 0, v)
            elif at == 1:
                u = 1 - v
                wait(r4[r].at[u], sem4.at[r, u])
                step5(r, u, 0)
                step5(r, u, 1)
                if u:
                    send(s5[r], r5[r], sem5.at[r, 0], to)
            elif v == 1:
                wait(r4[r], sem4.at[r, 0])
                step5(r, 1, 0)
                step5(r, 1, 1)
                send(s5[r], r5[r], sem5.at[r, 0], to)
                step5(r, 0, 0)
                step5(r, 0, 1)

    for r in range(6):
        if zlast_at(r) == 2:
            wait(r5[r].at[1], sem5.at[r, 1])
        else:
            wait(r5[r], sem5.at[r, 0])
        s6[r][...] = (k5[r][1] + r5[r][1].astype(F32)).astype(BF16)
        send(s6[r], r6[r], sem6.at[r], device((bits_of(r)[5],), c))
    for r, (h, start, width) in enumerate(STREAMS):
        if zlast_at(r) == 2:
            wait(r5[r].at[0], sem5.at[r, 0])
        wait(r6[r], sem6.at[r])
        total = k5[r][0] + r5[r][0].astype(F32) + r6[r][...].astype(F32)
        out[16 * h : 16 * h + 16, :, start : start + width] = total.reshape(16, 8, width)

    for copy in sent:
        copy.wait_send()


def on_device(amplitudes, integrals, owner_order, screen_list, live_mask):
    rows, tiles, width = amplitudes.shape
    widths = [w for _, _, w in STREAMS]

    def group(lead, tail, dtype):
        return [pltpu.VMEM(lead + tail(w), dtype) for w in widths]

    two = (2,)
    raw = lambda w: (16, w)
    dense = lambda w: (128, w)
    scratch = [
        pltpu.VMEM((rows * tiles, width), BF16),
        pltpu.VMEM((4, width, width), BF16),
        pltpu.VMEM((20, rows, width), BF16),
        pltpu.VMEM((4, 8, rows, width), BF16),
        pltpu.VMEM(two * 8 + (16, width), BF16),
        pltpu.VMEM((12, 128, 256), BF16),
        *group(two * 7, raw, BF16),
        *group(two * 6, raw, BF16),
        *group(two * 6, raw, BF16),
        *group(two * 2, dense, BF16),
        *group(two * 2, dense, BF16),
        *group(two * 2, dense, F32),
        *group(two, dense, BF16),
        *group(two, dense, BF16),
        *group(two, dense, F32),
        *group((), dense, BF16),
        *group((), dense, BF16),
        pltpu.SemaphoreType.DMA((5,)),
        pltpu.SemaphoreType.DMA((4,)),
        pltpu.SemaphoreType.DMA((4,)),
        pltpu.SemaphoreType.DMA,
        *[pltpu.SemaphoreType.DMA((6, 2))] * 5,
        pltpu.SemaphoreType.DMA((6,)),
    ]
    smem = pl.BlockSpec(memory_space=pltpu.SMEM)
    hbm = pl.BlockSpec(memory_space=pl.ANY)
    return pl.pallas_call(
        kernel,
        out_shape=jax.ShapeDtypeStruct((rows, 8, width), F32),
        in_specs=[smem, smem, smem, hbm, hbm],
        out_specs=pl.BlockSpec(memory_space=pltpu.VMEM),
        scratch_shapes=scratch,
        cost_estimate=pl.CostEstimate(flops=13_000_000_000, bytes_accessed=12 << 20, transcendentals=0),
        compiler_params=pltpu.CompilerParams(
            collective_id=0, has_side_effects=True, vmem_limit_bytes=60 << 20
        ),
    )(owner_order, screen_list.T, live_mask.T, amplitudes.reshape(rows * tiles, width), integrals[0])


def solution(mesh):
    in_specs = (P("tile", None, None), P("tile", "rep", None, None), P(), P(), P())
    out_specs = P("tile", "rep", None)
    return jax.shard_map(
        on_device, mesh=mesh, in_specs=in_specs, out_specs=out_specs, check_vma=False
    )
```

```python
import functools

import jax
import jax.numpy as jnp
from jax import lax
from jax.experimental import pallas as pl
from jax.experimental.pallas import tpu as pltpu
from jax.sharding import PartitionSpec as P

MESH = pl.DeviceIdType.MESH
BF16, F32, I32 = jnp.bfloat16, jnp.float32, jnp.int32
NAT = ("x1", "x0", "z1", "z0", "y1", "y0")
ORDER = ("x0", "y0", "z0", "x1", "y1", "z1")
STREAMS = ((0, 0, 384), (0, 384, 384), (0, 768, 256), (1, 0, 384), (1, 384, 384), (1, 768, 256))
CHUNKS = (1, 2, 3, 0)


def bits_of(r):
    return [ORDER[(r + i) % 6] for i in range(6)]


def last_z(r):
    return [b for b in bits_of(r) if b[0] == "z"][1]


def gray(v):
    return v + v // 2 - 2 * (v // 3)


def left(r, used):
    gone = bits_of(r)[:used]
    return [b for b in NAT if b not in gone]


def view(ref, lead, names, fixed, tail=()):
    return ref.at[tuple(lead) + tuple(fixed[b] if b in fixed else slice(None) for b in names) + tuple(tail)]


def kernel(owner, screen, live, amp_hbm, int_hbm, out, amp, ints, ordered, column, pieces, weights, *rest):
    r1, r2, r3, s4, r4, k4, s5, r5, k5, s6, r6 = (rest[6 * i : 6 * i + 6] for i in range(11))
    load_sem, amp_sem, far_sem, send_sem, sem1, sem2, sem3, sem4, sem5, sem6 = rest[66:]
    x, t = lax.axis_index("rep"), lax.axis_index("tile")
    z, y, c = t // 8, (t // 2) % 4, t % 2
    g = {"x": gray(x), "y": gray(y), "z": gray(z)}
    mine = {a + "1": g[a] // 2 for a in g} | {a + "0": g[a] % 2 for a in g}
    other = {b: 1 - mine[b] for b in mine}

    def device(flips, core):
        at = {a: gray((other if a + "1" in flips else mine)[a + "1"] * 2 + (other if a + "0" in flips else mine)[a + "0"]) for a in g}
        return (at["z"] * 8 + at["y"] * 2 + core, at["x"])

    sent = []

    def send(src, dst, sem, to):
        copy = pltpu.make_async_remote_copy(src, dst, send_sem, sem, device_id=to, device_id_type=MESH)
        copy.start()
        sent.append(copy)

    def wait(ref, sem):
        pltpu.make_async_copy(ref, ref, sem).wait()

    load_amp = pltpu.make_async_copy(amp_hbm, amp, load_sem.at[0])
    load_amp.start()
    load_ints = [pltpu.make_async_copy(int_hbm.at[j], ints.at[j], load_sem.at[1 + j]) for j in range(4)]

    barrier = pltpu.get_barrier_semaphore()

    @pl.loop(1, 32)
    def _(k):
        to = ((z + k // 8) % 4) * 8 + ((y + (k // 2) % 4) % 4) * 2 + (c + k) % 2
        pl.semaphore_signal(barrier, inc=1, device_id=(to, x), device_id_type=MESH)

    for b in ("x0", "x1"):
        for core in range(2):
            pl.semaphore_signal(barrier, inc=1, device_id=device((b,), core), device_id_type=MESH)
    pl.semaphore_signal(barrier, inc=1, device_id=device(("x0", "x1"), c), device_id_type=MESH)

    def far(n):
        return ((2, x // 2), (2, 2 + x // 2), (1, 2 - x // 2), (3, 2 + x // 2))[n] + (x % 2,)

    load_amp.wait()
    for load in load_ints:
        load.start()
    away = lax.broadcasted_iota(I32, (32, 1024), 1) - 32 * lax.broadcasted_iota(I32, (32, 1024), 0)
    own_row = g["y"] * 2 + c
    near = [(dz, dy, dc) for dz, dy in ((1, 0), (1, 3), (3, 0), (3, 1), (0, 1), (0, 3), (0, 0), (0, 2)) for dc in (0, 1)]
    blocks = [far(n) for n in (2, 3, 0, 1)] + near
    for first in (0, 8, 16):
        some = blocks[first : first + 8]
        to = [((z + dz) % 4) * 8 + ((y + dy) % 4) * 2 + (c + dc) % 2 for dz, dy, dc in some]
        pick = [jnp.where(away == owner[p], 1.0, 0.0).astype(BF16) for p in to]
        pick = jnp.concatenate(pick, axis=0)
        for n in range(2):
            got = jnp.dot(pick, amp[:, n * 512 : n * 512 + 512], preferred_element_type=F32)
            ordered[first : first + len(some), :, n * 512 : n * 512 + 512] = got.astype(BF16).reshape(len(some), 32, 512)
        if first == 0:
            pl.semaphore_wait(barrier, 36)
        for i, p in enumerate(to):
            src, dst = ordered.at[first + i], column.at[g["z"], own_row]
            if some[i] == (0, 0, 0):
                pltpu.make_async_copy(src, dst, amp_sem.at[g["z"]]).start()
            elif first == 0 and i < 4:
                send(src, dst, far_sem.at[(2, 3, 0, 1)[i]], (p, x))
            else:
                send(src, dst, amp_sem.at[g["z"]], (p, x))

    lane = lax.broadcasted_iota(I32, (8, 256), 1)
    bin_of_row = lax.broadcasted_iota(I32, (8, 256), 0)
    for r in range(6):
        e = bits_of(r)
        x_left = [b for b in e[3:] if b[0] == "x"][0]
        for f in range(2):
            want = dict(mine)
            if f:
                want[x_left] = other[x_left]
            block = gray(want["x1"] * 2 + want["x0"])
            label = jnp.full((8, 256), -1, I32)
            for s in range(16):
                flips = [e[2 - i] for i in range(3) if (s >> (3 - i)) & 1]
                tile, rep = device(flips, s & 1)
                slot = rep * 4 + block
                found = jnp.where(live[slot, tile] != 0, screen[slot, tile] - 8 * block, -1)
                label = jnp.where(lane // 16 == s, found, label)
            hit = label == bin_of_row
            rows = [jnp.where(hit & (lane % 16 == m), 1.0, 0.0).astype(F32) for m in range(16)]
            weights[2 * r + f] = jnp.concatenate(rows, axis=0).astype(BF16)

    for n in (2, 3, 0, 1):
        dz, dy, dc = far(n)
        gz = gray((z - dz + 4) % 4)
        block = column.at[gz, gray((y - dy + 4) % 4) * 2 + (c + dc) % 2]
        wait(block, far_sem.at[n])
        for dx in (1, 3, 2):
            send(block, block, amp_sem.at[gz], (t, (x + dx) % 4))

    for load in load_ints:
        load.wait()

    for k in CHUNKS:
        zv = {"z1": (other if k >> 1 else mine)["z1"], "z0": (other if k & 1 else mine)["z0"]}
        gz = zv["z1"] * 2 + zv["z0"]
        wait(column.at[gz, pl.ds(0, (8, 7, 7, 6)[k])], amp_sem.at[gz])

        @pl.loop(0, 4)
        def _(j):
            left_side = column[gz].reshape(256, 1024)
            got = jnp.dot(left_side, ints[j], preferred_element_type=F32).astype(BF16)
            gj = gray(j)
            pieces[gj // 2, gj % 2, zv["z1"], zv["z0"]] = got.reshape(2, 2, 2, 2, 16, 1024)

        for r, (h, start, width) in enumerate(STREAMS):
            e1, zl = bits_of(r)[0], last_z(r)
            v = k >> 1 if zl == "z1" else k & 1
            sem = sem1.at[r, v]
            cols = pl.ds(start, width)
            flip_z = {"z0": k & 1, "z1": k >> 1}
            names = left(r, 1)

            def part(e1_value, core):
                return view(pieces, (), NAT, {e1: e1_value} | zv, (core, h, slice(None), cols))

            def place(a):
                return view(r1[r], (a, c), names, {b: n for b, n in zv.items() if b != e1})

            if e1[0] != "z" or flip_z[e1]:
                for core in range(2):
                    send(part(other[e1], core), place(1), sem, device((e1,), core))
            if e1[0] != "z" or not flip_z[e1]:
                send(part(mine[e1], 1 - c), place(0), sem, device((), 1 - c))
                pltpu.make_async_copy(part(mine[e1], c), place(0), sem).start()

    def keys(r):
        e, zl = bits_of(r), last_z(r)
        return (zl, e[4]) if zl == e[3] else (zl, e[3])

    def pick_part(r, v, u):
        first, second = keys(r)
        return {first: (other if v else mine)[first], second: (other if u else mine)[second]}

    every = slice(None)
    for v in (1, 0):
        for r in range(6):
            e1, e2, e3 = bits_of(r)[:3]
            zl = last_z(r)
            wait(view(r1[r], (every, every), left(r, 1), {zl: (other if v else mine)[zl]}), sem1.at[r, v])
            for u in (1, 0):
                fix = pick_part(r, v, u)
                send(
                    view(r1[r], (every, every), left(r, 1), {e2: other[e2]} | fix),
                    view(r2[r], (every, every), left(r, 2), fix),
                    sem2.at[r, 2 * v + u],
                    device((e2,), c),
                )
        for r in range(6):
            e1, e2, e3 = bits_of(r)[:3]
            for u in (1, 0):
                fix = pick_part(r, v, u)
                send(
                    view(r1[r], (every, every), left(r, 1), {e2: mine[e2], e3: other[e3]} | fix),
                    view(r3[r], (0, every, every), left(r, 3), fix),
                    sem3.at[r, 2 * v + u],
                    device((e3,), c),
                )

    def step3(r, v, u):
        e1, e2, e3 = bits_of(r)[:3]
        fix = pick_part(r, v, u)
        wait(view(r2[r], (every, every), left(r, 2), fix), sem2.at[r, 2 * v + u])
        send(
            view(r2[r], (every, every), left(r, 2), {e3: other[e3]} | fix),
            view(r3[r], (1, every, every), left(r, 3), fix),
            sem3.at[r, 2 * v + u],
            device((e3,), c),
        )

    def step4(r, v, u):
        e = bits_of(r)
        first, second = keys(r)
        wait(view(r3[r], (every,) * 3, left(r, 3), pick_part(r, v, u)), sem3.at[r, 2 * v + u])
        x_left = [b for b in e[3:] if b[0] == "x"][0]
        for w in range(2):
            flip = {b: w for b in e[3:]} | {first: v, second: u}
            here = {b: (other if flip[b] else mine)[b] for b in e[3:]} | {e[1]: mine[e[1]], e[2]: mine[e[2]]}
            blocks = []
            for ref, lead in ((r1[r], 0), (r2[r], 0), (r3[r], 1)):
                for a in range(4 << lead):
                    front = ((a >> 2,) if lead else ()) + ((a >> 1) & 1, a & 1)
                    used = 3 if lead else (1 if ref is r1[r] else 2)
                    blocks.append(ref[front + tuple(here[b] for b in left(r, used))])
            table = weights[2 * r + flip[x_left]]
            binned = jnp.dot(table, jnp.concatenate(blocks, axis=0), preferred_element_type=F32)
            f4, f5, f6 = (flip[b] for b in e[3:])
            if f4:
                s4[r][f5, f6] = binned.astype(BF16)
            else:
                k4[r][f5, f6] = binned
        to = device((e[3],), c)
        if first == e[3] and v:
            send(s4[r].at[u], r4[r].at[u], sem4.at[r, u], to)
        elif first == e[4] and u:
            send(s4[r].at[v], r4[r].at[v], sem4.at[r, v], to)
        elif first == e[5] and u:
            send(s4[r].at[:, v], r4[r].at[:, v], sem4.at[r, v], to)

    def add5(r, f5, f6):
        total = k4[r][f5, f6] + r4[r][f5, f6].astype(F32)
        if f5:
            s5[r][f6] = total.astype(BF16)
        else:
            k5[r][f6] = total

    def step5(r, v, u):
        e, first = bits_of(r), keys(r)[0]
        to = device((e[4],), c)
        if first == e[3] and not v:
            wait(r4[r].at[u], sem4.at[r, u])
            add5(r, u, 0)
            add5(r, u, 1)
            if u:
                send(s5[r], r5[r], sem5.at[r, 0], to)
        elif first == e[4] and not u:
            wait(r4[r].at[v], sem4.at[r, v])
            add5(r, v, 0)
            add5(r, v, 1)
            if v:
                send(s5[r], r5[r], sem5.at[r, 0], to)
        elif first == e[5] and not u:
            wait(r4[r].at[:, v], sem4.at[r, v])
            add5(r, 1, v)
            send(s5[r].at[v], r5[r].at[v], sem5.at[r, v], to)
            add5(r, 0, v)

    parts = ((1, 1), (1, 0), (0, 1), (0, 0))
    for n in range(6):
        for r in range(6):
            if n < 4:
                step3(r, *parts[n])
        for r in range(6):
            if 1 < n:
                step4(r, *parts[n - 2])
        for r in range(6):
            if 1 < n:
                step5(r, *parts[n - 2])

    for r in range(6):
        if keys(r)[0] == bits_of(r)[5]:
            wait(r5[r].at[1], sem5.at[r, 1])
        else:
            wait(r5[r], sem5.at[r, 0])
        s6[r][...] = (k5[r][1] + r5[r][1].astype(F32)).astype(BF16)
        send(s6[r], r6[r], sem6.at[r], device((bits_of(r)[5],), c))
    for r, (h, start, width) in enumerate(STREAMS):
        if keys(r)[0] == bits_of(r)[5]:
            wait(r5[r].at[0], sem5.at[r, 0])
        wait(r6[r], sem6.at[r])
        total = k5[r][0] + r5[r][0].astype(F32) + r6[r][...].astype(F32)
        out[16 * h : 16 * h + 16, :, start : start + width] = total.reshape(16, 8, width)

    for copy in sent:
        copy.wait_send()


def on_device(amplitudes, integrals, owner_order, screen_list, live_mask):
    rows, tiles, width = amplitudes.shape
    widths = [w for _, _, w in STREAMS]

    def group(lead, tail, dtype):
        return [pltpu.VMEM(lead + tail(w), dtype) for w in widths]

    two = (2,)
    raw = lambda w: (16, w)
    dense = lambda w: (128, w)
    scratch = [
        pltpu.VMEM((rows * tiles, width), BF16),
        pltpu.VMEM((4, width, width), BF16),
        pltpu.VMEM((20, rows, width), BF16),
        pltpu.VMEM((4, 8, rows, width), BF16),
        pltpu.VMEM(two * 8 + (16, width), BF16),
        pltpu.VMEM((12, 128, 256), BF16),
        *group(two * 7, raw, BF16),
        *group(two * 6, raw, BF16),
        *group(two * 6, raw, BF16),
        *group(two * 2, dense, BF16),
        *group(two * 2, dense, BF16),
        *group(two * 2, dense, F32),
        *group(two, dense, BF16),
        *group(two, dense, BF16),
        *group(two, dense, F32),
        *group((), dense, BF16),
        *group((), dense, BF16),
        pltpu.SemaphoreType.DMA((5,)),
        pltpu.SemaphoreType.DMA((4,)),
        pltpu.SemaphoreType.DMA((4,)),
        pltpu.SemaphoreType.DMA,
        pltpu.SemaphoreType.DMA((6, 2)),
        *[pltpu.SemaphoreType.DMA((6, 4))] * 2,
        *[pltpu.SemaphoreType.DMA((6, 2))] * 2,
        pltpu.SemaphoreType.DMA((6,)),
    ]
    smem = pl.BlockSpec(memory_space=pltpu.SMEM)
    hbm = pl.BlockSpec(memory_space=pl.ANY)
    return pl.pallas_call(
        kernel,
        out_shape=jax.ShapeDtypeStruct((rows, 8, width), F32),
        in_specs=[smem, smem, smem, hbm, hbm],
        out_specs=pl.BlockSpec(memory_space=pltpu.VMEM),
        scratch_shapes=scratch,
        cost_estimate=pl.CostEstimate(flops=13_000_000_000, bytes_accessed=12 << 20, transcendentals=0),
        compiler_params=pltpu.CompilerParams(
            collective_id=0, has_side_effects=True, vmem_limit_bytes=60 << 20
        ),
    )(owner_order, screen_list.T, live_mask.T, amplitudes.reshape(rows * tiles, width), integrals[0])


def solution(mesh):
    in_specs = (P("tile", None, None), P("tile", "rep", None, None), P(), P(), P())
    out_specs = P("tile", "rep", None)
    return jax.shard_map(
        on_device, mesh=mesh, in_specs=in_specs, out_specs=out_specs, check_vma=False
    )
```

```python
import jax
import jax.numpy as jnp
from jax import lax
from jax.experimental import pallas as pl
from jax.experimental.pallas import tpu as pltpu
from jax.sharding import PartitionSpec as P

MESH = pl.DeviceIdType.MESH
BF16, F32, I32 = jnp.bfloat16, jnp.float32, jnp.int32
NAT = ("x1", "x0", "z1", "z0", "y1", "y0")
ORDER = ("x0", "y0", "z0", "x1", "y1", "z1")
STREAMS = ((0, 0, 384, 0), (0, 384, 384, 1), (0, 768, 256, 2), (1, 0, 384, 0), (1, 384, 384, 1), (1, 768, 256, 2))
CHUNKS = (1, 2, 3, 0)


def a_bits(q):
    return [axis + str(q) for axis in "xyz"]


def b_bits(r):
    q, first = STREAMS[r][0], STREAMS[r][3]
    return ["xyz"[(first + i) % 3] + str(1 - q) for i in range(3)]


def tables(r):
    ahead = b_bits(r)[0][0] == "x"
    return [(r, a, f) for a in range(2) for f in range(1 if ahead else 2)]


TABLES = [key for r in range(6) for key in tables(r)]


def gray(v):
    return v + v // 2 - 2 * (v // 3)


def view(ref, lead, names, fixed, tail=()):
    return ref.at[tuple(lead) + tuple(fixed[b] if b in fixed else slice(None) for b in names) + tuple(tail)]


def kernel(owner, screen, live, amp_hbm, int_hbm, out, amp, ints, ordered, column, pieces, weights, *rest):
    r1 = rest[:2]
    r3, s4, r4, k4, s5, r5, k5, s6, r6 = (rest[2 + 6 * i : 8 + 6 * i] for i in range(9))
    load_sem, amp_sem, far_sem, send_sem, sem1, sem3, sem4, sem5, sem6 = rest[56:]
    x, t = lax.axis_index("rep"), lax.axis_index("tile")
    z, y, c = t // 8, (t // 2) % 4, t % 2
    g = {"x": gray(x), "y": gray(y), "z": gray(z)}
    mine = {a + "1": g[a] // 2 for a in g} | {a + "0": g[a] % 2 for a in g}
    other = {b: 1 - mine[b] for b in mine}

    def device(flips, core):
        at = {a: gray((other if a + "1" in flips else mine)[a + "1"] * 2 + (other if a + "0" in flips else mine)[a + "0"]) for a in g}
        return (at["z"] * 8 + at["y"] * 2 + core, at["x"])

    sent = []

    def send(src, dst, sem, to):
        copy = pltpu.make_async_remote_copy(src, dst, send_sem, sem, device_id=to, device_id_type=MESH)
        copy.start()
        sent.append(copy)

    def wait(ref, sem):
        pltpu.make_async_copy(ref, ref, sem).wait()

    load_amp = pltpu.make_async_copy(amp_hbm, amp, load_sem.at[0])
    load_amp.start()
    load_ints = [pltpu.make_async_copy(int_hbm.at[j], ints.at[j], load_sem.at[1 + j]) for j in range(4)]

    barrier = pltpu.get_barrier_semaphore()

    @pl.loop(1, 32)
    def _(k):
        to = ((z + k // 8) % 4) * 8 + ((y + (k // 2) % 4) % 4) * 2 + (c + k) % 2
        pl.semaphore_signal(barrier, inc=1, device_id=(to, x), device_id_type=MESH)

    for b in ("x0", "x1"):
        for core in range(2):
            pl.semaphore_signal(barrier, inc=1, device_id=device((b,), core), device_id_type=MESH)
    pl.semaphore_signal(barrier, inc=1, device_id=device(("x0", "x1"), c), device_id_type=MESH)
    for q in range(2):
        pl.semaphore_signal(barrier, inc=1, device_id=device(a_bits(q), c), device_id_type=MESH)

    def far(n):
        return ((2, x // 2), (2, 2 + x // 2), (1, 2 - x // 2), (3, 2 + x // 2))[n] + (x % 2,)

    load_amp.wait()
    for load in load_ints:
        load.start()
    away = lax.broadcasted_iota(I32, (32, 1024), 1) - 32 * lax.broadcasted_iota(I32, (32, 1024), 0)
    own_row = g["y"] * 2 + c
    near = [(dz, dy, dc) for dz, dy in ((1, 0), (1, 3), (3, 0), (3, 1), (0, 1), (0, 3), (0, 0), (0, 2)) for dc in (0, 1)]
    blocks = [far(n) for n in (2, 3, 0, 1)] + near
    for first in (0, 8, 16):
        some = blocks[first : first + 8]
        to = [((z + dz) % 4) * 8 + ((y + dy) % 4) * 2 + (c + dc) % 2 for dz, dy, dc in some]
        pick = [jnp.where(away == owner[p], 1.0, 0.0).astype(BF16) for p in to]
        pick = jnp.concatenate(pick, axis=0)
        for n in range(2):
            got = jnp.dot(pick, amp[:, n * 512 : n * 512 + 512], preferred_element_type=F32)
            ordered[first : first + len(some), :, n * 512 : n * 512 + 512] = got.astype(BF16).reshape(len(some), 32, 512)
        if first == 0:
            pl.semaphore_wait(barrier, 38)
        for i, p in enumerate(to):
            src, dst = ordered.at[first + i], column.at[g["z"], own_row]
            if some[i] == (0, 0, 0):
                pltpu.make_async_copy(src, dst, amp_sem.at[g["z"]]).start()
            elif first == 0 and i < 4:
                send(src, dst, far_sem.at[(2, 3, 0, 1)[i]], (p, x))
            else:
                send(src, dst, amp_sem.at[g["z"]], (p, x))

    lane = lax.broadcasted_iota(I32, (8, 256), 1)
    bin_of_row = lax.broadcasted_iota(I32, (8, 256), 0)
    for n, (r, a, f) in enumerate(TABLES):
        q, b1 = STREAMS[r][0], b_bits(r)[0]
        xa, xb = "x" + str(q), "x" + str(1 - q)
        want = {xa: (other if a else mine)[xa], xb: (other if f else mine)[xb]}
        block = gray(want["x1"] * 2 + want["x0"])
        label = jnp.full((8, 256), -1, I32)
        for s in range(16):
            chip = (s >> 1) & 3
            tile, rep = device(([b1] if s >> 3 else []) + ([a_bits(q)[chip - 1]] if chip else []), s & 1)
            slot = rep * 4 + block
            found = jnp.where(live[slot, tile] != 0, screen[slot, tile] - 8 * block, -1)
            label = jnp.where(lane // 16 == s, found, label)
        hit = label == bin_of_row
        rows = [jnp.where(hit & (lane % 16 == m), 1.0, 0.0).astype(F32) for m in range(16)]
        weights[n] = jnp.concatenate(rows, axis=0).astype(BF16)

    for n in (2, 3, 0, 1):
        dz, dy, dc = far(n)
        gz = gray((z - dz + 4) % 4)
        block = column.at[gz, gray((y - dy + 4) % 4) * 2 + (c + dc) % 2]
        wait(block, far_sem.at[n])
        for dx in (1, 3, 2):
            send(block, block, amp_sem.at[gz], (t, (x + dx) % 4))

    for load in load_ints:
        load.wait()

    for k in CHUNKS:
        zv = {"z1": (other if k >> 1 else mine)["z1"], "z0": (other if k & 1 else mine)["z0"]}
        gz = zv["z1"] * 2 + zv["z0"]
        wait(column.at[gz, pl.ds(0, (8, 7, 7, 6)[k])], amp_sem.at[gz])

        @pl.loop(0, 4)
        def _(j):
            left_side = column[gz].reshape(256, 1024)
            got = jnp.dot(left_side, ints[j], preferred_element_type=F32).astype(BF16)
            gj = gray(j)
            pieces[gj // 2, gj % 2, zv["z1"], zv["z0"]] = got.reshape(2, 2, 2, 2, 16, 1024)

        flip_z = {"z0": k & 1, "z1": k >> 1}
        for q in range(2):
            xa, ya, za = a_bits(q)
            zb = "z" + str(1 - q)
            f = flip_z[za]
            sem = sem1.at[q, flip_z[zb]]

            def part(fx, fy, core):
                at = {xa: (other if fx else mine)[xa], ya: (other if fy else mine)[ya]} | zv
                return view(pieces, (), NAT, at, (core, q))

            def place(chip, a):
                return r1[q].at[chip, c, a, :, zv[zb], :]

            for core in range(2):
                send(part(1 - f, f, core), place(1, f), sem, device((xa,), core))
                send(part(f, 1 - f, core), place(2, f), sem, device((ya,), core))
                send(part(1 - f, 1 - f, core), place(3, 1 - f), sem, device((za,), core))
            send(part(f, f, 1 - c), place(0, f), sem, device((), 1 - c))
            pltpu.make_async_copy(part(f, f, c), place(0, f), sem).start()

    every = slice(None)

    def where(r, f1, f2, f3):
        b1, b2, b3 = b_bits(r)
        return {b: (other if f else mine)[b] for b, f in ((b1, f1), (b2, f2), (b3, f3))}

    def in_r1(r, at):
        q = STREAMS[r][0]
        return tuple(at[axis + str(1 - q)] for axis in "xzy")

    def in_r3(r, at):
        first = b_bits(r)[0]
        return tuple(at[b] for b in (axis + str(1 - STREAMS[r][0]) for axis in "xzy") if b != first)

    def columns(r):
        return pl.ds(STREAMS[r][1], STREAMS[r][2])

    def z_at(r):
        return [b[0] for b in b_bits(r)].index("z")

    halves = ((1, 1), (1, 0), (0, 1), (0, 0))

    def step3(r, a, f2, f3):
        at = where(r, 1, f2, f3)
        src = r1[STREAMS[r][0]].at[(every, every, a) + in_r1(r, at) + (every, columns(r))]
        dst = r3[r].at[(every, every, a) + in_r3(r, at)]
        send(src, dst, sem3.at[r, 4 * a + 2 * f2 + f3], device((b_bits(r)[0],), c))

    for v in (1, 0):
        for q in range(2):
            zb = "z" + str(1 - q)
            wait(r1[q].at[:, :, :, :, (other if v else mine)[zb], :], sem1.at[q, v])
            for a in (1, 0):
                for f2, f3 in halves:
                    for r in range(3 * q, 3 * q + 3):
                        if (1, f2, f3)[z_at(r)] == v:
                            step3(r, a, f2, f3)

    def step4(r, a, f2, f3):
        q = STREAMS[r][0]
        at = where(r, 0, f2, f3)
        wait(r3[r].at[(every, every, a) + in_r3(r, at)], sem3.at[r, 4 * a + 2 * f2 + f3])
        fx = {b_bits(r)[1]: f2, b_bits(r)[2]: f3}.get("x" + str(1 - q), 0)
        blocks = []
        for chip in range(4):
            for core in range(2):
                blocks.append(r1[q][(chip, core, a) + in_r1(r, at) + (every, columns(r))])
        for chip in range(4):
            for core in range(2):
                blocks.append(r3[r][(chip, core, a) + in_r3(r, at)])
        table = weights[TABLES.index((r, a, fx))]
        binned = jnp.dot(table, jnp.concatenate(blocks, axis=0), preferred_element_type=F32)
        if f2:
            s4[r][f3, a] = binned.astype(BF16)
            send(s4[r].at[f3, a], r4[r].at[f3, a], sem4.at[r, 2 * a + f3], device((b_bits(r)[1],), c))
        else:
            k4[r][f3, a] = binned

    def step5(r, a, f3):
        wait(r4[r].at[f3, a], sem4.at[r, 2 * a + f3])
        total = k4[r][f3, a] + r4[r][f3, a].astype(F32)
        if f3:
            s5[r][a] = total.astype(BF16)
            send(s5[r].at[a], r5[r].at[a], sem5.at[r, a], device((b_bits(r)[2],), c))
        else:
            k5[r][a] = total

    def home(r):
        wait(r5[r].at[1], sem5.at[r, 1])
        s6[r][...] = (k5[r][1] + r5[r][1].astype(F32)).astype(BF16)
        send(s6[r], r6[r], sem6.at[r], device(a_bits(STREAMS[r][0]), c))

    for a in (1, 0):
        for n, (f2, f3) in enumerate(halves):
            for r in range(6):
                step4(r, a, f2, f3)
            if f2 == 0:
                for r in range(6):
                    step5(r, a, f3)
            if (a, n) == (0, 1):
                for r in range(6):
                    home(r)
    for r, (q, start, width, _) in enumerate(STREAMS):
        wait(r5[r].at[0], sem5.at[r, 0])
        wait(r6[r], sem6.at[r])
        total = k5[r][0] + r5[r][0].astype(F32) + r6[r][...].astype(F32)
        out[16 * q : 16 * q + 16, :, start : start + width] = total.reshape(16, 8, width)

    for copy in sent:
        copy.wait_send()


def on_device(amplitudes, integrals, owner_order, screen_list, live_mask):
    rows, tiles, width = amplitudes.shape
    widths = [w for _, _, w, _ in STREAMS]

    def group(lead, tail, dtype):
        return [pltpu.VMEM(lead + tail(w), dtype) for w in widths]

    two = (2,)
    raw = lambda w: (16, w)
    dense = lambda w: (128, w)
    scratch = [
        pltpu.VMEM((rows * tiles, width), BF16),
        pltpu.VMEM((4, width, width), BF16),
        pltpu.VMEM((20, rows, width), BF16),
        pltpu.VMEM((4, 8, rows, width), BF16),
        pltpu.VMEM(two * 8 + (16, width), BF16),
        pltpu.VMEM((len(TABLES), 128, 256), BF16),
        *[pltpu.VMEM((4, 2, 2, 2, 2, 2, 16, width), BF16)] * 2,
        *group((4, 2, 2, 2, 2), raw, BF16),
        *group(two * 2, dense, BF16),
        *group(two * 2, dense, BF16),
        *group(two * 2, dense, F32),
        *group(two, dense, BF16),
        *group(two, dense, BF16),
        *group(two, dense, F32),
        *group((), dense, BF16),
        *group((), dense, BF16),
        pltpu.SemaphoreType.DMA((5,)),
        pltpu.SemaphoreType.DMA((4,)),
        pltpu.SemaphoreType.DMA((4,)),
        pltpu.SemaphoreType.DMA,
        pltpu.SemaphoreType.DMA((2, 2)),
        pltpu.SemaphoreType.DMA((6, 8)),
        pltpu.SemaphoreType.DMA((6, 4)),
        pltpu.SemaphoreType.DMA((6, 2)),
        pltpu.SemaphoreType.DMA((6,)),
    ]
    smem = pl.BlockSpec(memory_space=pltpu.SMEM)
    hbm = pl.BlockSpec(memory_space=pl.ANY)
    return pl.pallas_call(
        kernel,
        out_shape=jax.ShapeDtypeStruct((rows, 8, width), F32),
        in_specs=[smem, smem, smem, hbm, hbm],
        out_specs=pl.BlockSpec(memory_space=pltpu.VMEM),
        scratch_shapes=scratch,
        cost_estimate=pl.CostEstimate(flops=13_000_000_000, bytes_accessed=12 << 20, transcendentals=0),
        compiler_params=pltpu.CompilerParams(
            collective_id=0, has_side_effects=True, vmem_limit_bytes=60 << 20
        ),
    )(owner_order, screen_list.T, live_mask.T, amplitudes.reshape(rows * tiles, width), integrals[0])


def solution(mesh):
    in_specs = (P("tile", None, None), P("tile", "rep", None, None), P(), P(), P())
    out_specs = P("tile", "rep", None)
    return jax.shard_map(
        on_device, mesh=mesh, in_specs=in_specs, out_specs=out_specs, check_vma=False
    )
```

```python
import jax
import jax.numpy as jnp
from jax import lax
from jax.experimental import pallas as pl
from jax.experimental.pallas import tpu as pltpu
from jax.sharding import PartitionSpec as P

MESH = pl.DeviceIdType.MESH
BF16, F32, I32 = jnp.bfloat16, jnp.float32, jnp.int32
NAT = ("x1", "x0", "z1", "z0", "y1", "y0")
ORDER = ("x0", "y0", "z0", "x1", "y1", "z1")
STREAMS = ((0, 0, 384, 0), (0, 384, 384, 1), (0, 768, 256, 2), (1, 0, 384, 0), (1, 384, 384, 1), (1, 768, 256, 2))
CHUNKS = (1, 2, 3, 0)


def a_bits(q):
    return [axis + str(q) for axis in "xyz"]


def b_bits(r):
    q, first = STREAMS[r][0], STREAMS[r][3]
    return ["xyz"[(first + i) % 3] + str(1 - q) for i in range(3)]


def tables(r):
    ahead = b_bits(r)[0][0] == "x"
    return [(r, a, f) for a in range(2) for f in range(1 if ahead else 2)]


TABLES = [key for r in range(6) for key in tables(r)]


def gray(v):
    return v + v // 2 - 2 * (v // 3)


def view(ref, lead, names, fixed, tail=()):
    return ref.at[tuple(lead) + tuple(fixed[b] if b in fixed else slice(None) for b in names) + tuple(tail)]


def kernel(owner, screen, live, amp_hbm, int_hbm, out, amp, ints, ordered, column, pieces, weights, *rest):
    r1 = rest[:2]
    r3, s4, r4, k4, s5, r5, k5, s6, r6 = (rest[2 + 6 * i : 8 + 6 * i] for i in range(9))
    load_sem, amp_sem, far_sem, send_sem, sem1, sem3, sem4, sem5, sem6 = rest[56:]
    x, t = lax.axis_index("rep"), lax.axis_index("tile")
    z, y, c = t // 8, (t // 2) % 4, t % 2
    g = {"x": gray(x), "y": gray(y), "z": gray(z)}
    mine = {a + "1": g[a] // 2 for a in g} | {a + "0": g[a] % 2 for a in g}
    other = {b: 1 - mine[b] for b in mine}

    def device(flips, core):
        at = {a: gray((other if a + "1" in flips else mine)[a + "1"] * 2 + (other if a + "0" in flips else mine)[a + "0"]) for a in g}
        return (at["z"] * 8 + at["y"] * 2 + core, at["x"])

    sent = []

    def send(src, dst, sem, to):
        copy = pltpu.make_async_remote_copy(src, dst, send_sem, sem, device_id=to, device_id_type=MESH)
        copy.start()
        sent.append(copy)

    def wait(ref, sem):
        pltpu.make_async_copy(ref, ref, sem).wait()

    load_amp = pltpu.make_async_copy(amp_hbm, amp, load_sem.at[0])
    load_amp.start()
    load_ints = [pltpu.make_async_copy(int_hbm.at[j], ints.at[j], load_sem.at[1 + j]) for j in range(4)]

    barrier = pltpu.get_barrier_semaphore()

    @pl.loop(1, 32)
    def _(k):
        to = ((z + k // 8) % 4) * 8 + ((y + (k // 2) % 4) % 4) * 2 + (c + k) % 2
        pl.semaphore_signal(barrier, inc=1, device_id=(to, x), device_id_type=MESH)

    for b in ("x0", "x1"):
        for core in range(2):
            pl.semaphore_signal(barrier, inc=1, device_id=device((b,), core), device_id_type=MESH)
    pl.semaphore_signal(barrier, inc=1, device_id=device(("x0", "x1"), c), device_id_type=MESH)
    for q in range(2):
        pl.semaphore_signal(barrier, inc=1, device_id=device(a_bits(q), c), device_id_type=MESH)

    def far(n):
        return ((2, x // 2), (2, 2 + x // 2), (1, 2 - x // 2), (3, 2 + x // 2))[n] + (x % 2,)

    load_amp.wait()
    for load in load_ints:
        load.start()
    away = lax.broadcasted_iota(I32, (32, 1024), 1) - 32 * lax.broadcasted_iota(I32, (32, 1024), 0)
    own_row = g["y"] * 2 + c
    near = [(dz, dy, dc) for dz, dy in ((1, 0), (1, 3), (3, 0), (3, 1), (0, 1), (0, 3), (0, 0), (0, 2)) for dc in (0, 1)]
    blocks = [far(n) for n in (2, 3, 0, 1)] + near
    for first in (0, 8, 16):
        some = blocks[first : first + 8]
        to = [((z + dz) % 4) * 8 + ((y + dy) % 4) * 2 + (c + dc) % 2 for dz, dy, dc in some]
        pick = [jnp.where(away == owner[p], 1.0, 0.0).astype(BF16) for p in to]
        pick = jnp.concatenate(pick, axis=0)
        for n in range(2):
            got = jnp.dot(pick, amp[:, n * 512 : n * 512 + 512], preferred_element_type=F32)
            ordered[first : first + len(some), :, n * 512 : n * 512 + 512] = got.astype(BF16).reshape(len(some), 32, 512)
        if first == 0:
            pl.semaphore_wait(barrier, 38)
        for i, p in enumerate(to):
            src, dst = ordered.at[first + i], column.at[g["z"], own_row]
            if some[i] == (0, 0, 0):
                pltpu.make_async_copy(src, dst, amp_sem.at[g["z"]]).start()
            elif first == 0 and i < 4:
                send(src, dst, far_sem.at[(2, 3, 0, 1)[i]], (p, x))
            else:
                send(src, dst, amp_sem.at[g["z"]], (p, x))

    lane = lax.broadcasted_iota(I32, (8, 256), 1)
    bin_of_row = lax.broadcasted_iota(I32, (8, 256), 0)
    for n, (r, a, f) in enumerate(TABLES):
        q, b1 = STREAMS[r][0], b_bits(r)[0]
        xa, xb = "x" + str(q), "x" + str(1 - q)
        want = {xa: (other if a else mine)[xa], xb: (other if f else mine)[xb]}
        block = gray(want["x1"] * 2 + want["x0"])
        label = jnp.full((8, 256), -1, I32)
        for s in range(16):
            chip = (s >> 1) & 3
            tile, rep = device(([b1] if s >> 3 else []) + ([a_bits(q)[chip - 1]] if chip else []), s & 1)
            slot = rep * 4 + block
            found = jnp.where(live[slot, tile] != 0, screen[slot, tile] - 8 * block, -1)
            label = jnp.where(lane // 16 == s, found, label)
        hit = label == bin_of_row
        rows = [jnp.where(hit & (lane % 16 == m), 1.0, 0.0).astype(F32) for m in range(16)]
        weights[n] = jnp.concatenate(rows, axis=0).astype(BF16)

    for n in (2, 3, 0, 1):
        dz, dy, dc = far(n)
        gz = gray((z - dz + 4) % 4)
        block = column.at[gz, gray((y - dy + 4) % 4) * 2 + (c + dc) % 2]
        wait(block, far_sem.at[n])
        for dx in (1, 3, 2):
            send(block, block, amp_sem.at[gz], (t, (x + dx) % 4))

    for load in load_ints:
        load.wait()

    for k in CHUNKS:
        zv = {"z1": (other if k >> 1 else mine)["z1"], "z0": (other if k & 1 else mine)["z0"]}
        gz = zv["z1"] * 2 + zv["z0"]
        wait(column.at[gz, pl.ds(0, (8, 7, 7, 6)[k])], amp_sem.at[gz])

        @pl.loop(0, 4)
        def _(j):
            left_side = column[gz].reshape(256, 1024)
            got = jnp.dot(left_side, ints[j], preferred_element_type=F32).astype(BF16)
            gj = gray(j)
            pieces[gj // 2, gj % 2, zv["z1"], zv["z0"]] = got.reshape(2, 2, 2, 2, 16, 1024)

        flip_z = {"z0": k & 1, "z1": k >> 1}
        for q in range(2):
            xa, ya, za = a_bits(q)
            zb = "z" + str(1 - q)
            f = flip_z[za]
            sem = sem1.at[q, flip_z[zb]]

            def part(fx, fy, core):
                at = {xa: (other if fx else mine)[xa], ya: (other if fy else mine)[ya]} | zv
                return view(pieces, (), NAT, at, (core, q))

            def place(chip, a):
                return r1[q].at[chip, c, a, :, zv[zb], :]

            for core in range(2):
                send(part(1 - f, f, core), place(1, f), sem, device((xa,), core))
                send(part(f, 1 - f, core), place(2, f), sem, device((ya,), core))
                send(part(1 - f, 1 - f, core), place(3, 1 - f), sem, device((za,), core))
            send(part(f, f, 1 - c), place(0, f), sem, device((), 1 - c))
            pltpu.make_async_copy(part(f, f, c), place(0, f), sem).start()

    every = slice(None)

    def where(r, f1, f2, f3):
        b1, b2, b3 = b_bits(r)
        return {b: (other if f else mine)[b] for b, f in ((b1, f1), (b2, f2), (b3, f3))}

    def in_r1(r, at):
        q = STREAMS[r][0]
        return tuple(at[axis + str(1 - q)] for axis in "xzy")

    def in_r3(r, at):
        first = b_bits(r)[0]
        return tuple(at[b] for b in (axis + str(1 - STREAMS[r][0]) for axis in "xzy") if b != first)

    def columns(r):
        return pl.ds(STREAMS[r][1], STREAMS[r][2])

    def z_at(r):
        return [b[0] for b in b_bits(r)].index("z")

    halves = ((1, 1), (1, 0), (0, 1), (0, 0))

    def step3(r, a, f2, f3):
        at = where(r, 1, f2, f3)
        src = r1[STREAMS[r][0]].at[(every, every, a) + in_r1(r, at) + (every, columns(r))]
        dst = r3[r].at[(every, every, a) + in_r3(r, at)]
        send(src, dst, sem3.at[r, 4 * a + 2 * f2 + f3], device((b_bits(r)[0],), c))

    for v in (1, 0):
        for q in range(2):
            zb = "z" + str(1 - q)
            wait(r1[q].at[:, :, :, :, (other if v else mine)[zb], :], sem1.at[q, v])
            for f2, f3 in halves:
                for r in range(3 * q, 3 * q + 3):
                    if (1, f2, f3)[z_at(r)] == v:
                        step3(r, 1, f2, f3)

    def step4(r, a, f2, f3):
        q = STREAMS[r][0]
        at = where(r, 0, f2, f3)
        wait(r3[r].at[(every, every, a) + in_r3(r, at)], sem3.at[r, 4 * a + 2 * f2 + f3])
        fx = {b_bits(r)[1]: f2, b_bits(r)[2]: f3}.get("x" + str(1 - q), 0)
        blocks = []
        for chip in range(4):
            for core in range(2):
                blocks.append(r1[q][(chip, core, a) + in_r1(r, at) + (every, columns(r))])
        for chip in range(4):
            for core in range(2):
                blocks.append(r3[r][(chip, core, a) + in_r3(r, at)])
        table = weights[TABLES.index((r, a, fx))]
        binned = jnp.dot(table, jnp.concatenate(blocks, axis=0), preferred_element_type=F32)
        if f2:
            s4[r][f3, a] = binned.astype(BF16)
            send(s4[r].at[f3, a], r4[r].at[f3, a], sem4.at[r, 2 * a + f3], device((b_bits(r)[1],), c))
        else:
            k4[r][f3, a] = binned

    def step5(r, a, f3):
        wait(r4[r].at[f3, a], sem4.at[r, 2 * a + f3])
        total = k4[r][f3, a] + r4[r][f3, a].astype(F32)
        if f3:
            s5[r][a] = total.astype(BF16)
            send(s5[r].at[a], r5[r].at[a], sem5.at[r, a], device((b_bits(r)[2],), c))
        else:
            k5[r][a] = total

    def home(r):
        wait(r5[r].at[1], sem5.at[r, 1])
        s6[r][...] = (k5[r][1] + r5[r][1].astype(F32)).astype(BF16)
        send(s6[r], r6[r], sem6.at[r], device(a_bits(STREAMS[r][0]), c))

    for n in range(1):
        for r in range(6):
            step3(r, 0, *halves[n])
    for a in (1, 0):
        for n, (f2, f3) in enumerate(halves):
            for r in range(6):
                step4(r, a, f2, f3)
            if f2 == 0:
                for r in range(6):
                    step5(r, a, f3)
            if a and n + 1 < 4:
                for r in range(6):
                    step3(r, 0, *halves[n + 1])
            if (a, n) == (0, 1):
                for r in range(6):
                    home(r)
    for r, (q, start, width, _) in enumerate(STREAMS):
        wait(r5[r].at[0], sem5.at[r, 0])
        wait(r6[r], sem6.at[r])
        total = k5[r][0] + r5[r][0].astype(F32) + r6[r][...].astype(F32)
        out[16 * q : 16 * q + 16, :, start : start + width] = total.reshape(16, 8, width)

    for copy in sent:
        copy.wait_send()


def on_device(amplitudes, integrals, owner_order, screen_list, live_mask):
    rows, tiles, width = amplitudes.shape
    widths = [w for _, _, w, _ in STREAMS]

    def group(lead, tail, dtype):
        return [pltpu.VMEM(lead + tail(w), dtype) for w in widths]

    two = (2,)
    raw = lambda w: (16, w)
    dense = lambda w: (128, w)
    scratch = [
        pltpu.VMEM((rows * tiles, width), BF16),
        pltpu.VMEM((4, width, width), BF16),
        pltpu.VMEM((20, rows, width), BF16),
        pltpu.VMEM((4, 8, rows, width), BF16),
        pltpu.VMEM(two * 8 + (16, width), BF16),
        pltpu.VMEM((len(TABLES), 128, 256), BF16),
        *[pltpu.VMEM((4, 2, 2, 2, 2, 2, 16, width), BF16)] * 2,
        *group((4, 2, 2, 2, 2), raw, BF16),
        *group(two * 2, dense, BF16),
        *group(two * 2, dense, BF16),
        *group(two * 2, dense, F32),
        *group(two, dense, BF16),
        *group(two, dense, BF16),
        *group(two, dense, F32),
        *group((), dense, BF16),
        *group((), dense, BF16),
        pltpu.SemaphoreType.DMA((5,)),
        pltpu.SemaphoreType.DMA((4,)),
        pltpu.SemaphoreType.DMA((4,)),
        pltpu.SemaphoreType.DMA,
        pltpu.SemaphoreType.DMA((2, 2)),
        pltpu.SemaphoreType.DMA((6, 8)),
        pltpu.SemaphoreType.DMA((6, 4)),
        pltpu.SemaphoreType.DMA((6, 2)),
        pltpu.SemaphoreType.DMA((6,)),
    ]
    smem = pl.BlockSpec(memory_space=pltpu.SMEM)
    hbm = pl.BlockSpec(memory_space=pl.ANY)
    return pl.pallas_call(
        kernel,
        out_shape=jax.ShapeDtypeStruct((rows, 8, width), F32),
        in_specs=[smem, smem, smem, hbm, hbm],
        out_specs=pl.BlockSpec(memory_space=pltpu.VMEM),
        scratch_shapes=scratch,
        cost_estimate=pl.CostEstimate(flops=13_000_000_000, bytes_accessed=12 << 20, transcendentals=0),
        compiler_params=pltpu.CompilerParams(
            collective_id=0, has_side_effects=True, vmem_limit_bytes=60 << 20
        ),
    )(owner_order, screen_list.T, live_mask.T, amplitudes.reshape(rows * tiles, width), integrals[0])


def solution(mesh):
    in_specs = (P("tile", None, None), P("tile", "rep", None, None), P(), P(), P())
    out_specs = P("tile", "rep", None)
    return jax.shard_map(
        on_device, mesh=mesh, in_specs=in_specs, out_specs=out_specs, check_vma=False
    )
```

```python
import jax
import jax.numpy as jnp
from jax import lax
from jax.experimental import pallas as pl
from jax.experimental.pallas import tpu as pltpu
from jax.sharding import PartitionSpec as P

MESH = pl.DeviceIdType.MESH
BF16, F32, I32 = jnp.bfloat16, jnp.float32, jnp.int32
NAT = ("x1", "x0", "z1", "z0", "y1", "y0")
ORDER = ("x0", "y0", "z0", "x1", "y1", "z1")
STREAMS = ((0, 0, 384, 0), (0, 384, 384, 1), (0, 768, 256, 2), (1, 0, 384, 0), (1, 384, 384, 1), (1, 768, 256, 2))
CHUNKS = (1, 2, 3, 0)


def a_bits(q):
    return [axis + str(q) for axis in "xyz"]


def b_bits(r):
    q, first = STREAMS[r][0], STREAMS[r][3]
    return ["xyz"[(first + i) % 3] + str(1 - q) for i in range(3)]


def tables(r):
    ahead = b_bits(r)[0][0] == "x"
    return [(r, a, f) for a in range(2) for f in range(1 if ahead else 2)]


TABLES = [key for r in range(6) for key in tables(r)]


def gray(v):
    return v + v // 2 - 2 * (v // 3)


def view(ref, lead, names, fixed, tail=()):
    return ref.at[tuple(lead) + tuple(fixed[b] if b in fixed else slice(None) for b in names) + tuple(tail)]


def kernel(owner, screen, live, amp_hbm, int_hbm, out, amp, ints, ordered, column, pieces, weights, *rest):
    r1 = rest[:2]
    r3, s4, r4, k4, s5, r5, k5, s6, r6 = (rest[2 + 6 * i : 8 + 6 * i] for i in range(9))
    load_sem, amp_sem, far_sem, send_sem, sem1, sem3, sem4, sem5, sem6 = rest[56:]
    x, t = lax.axis_index("rep"), lax.axis_index("tile")
    z, y, c = t // 8, (t // 2) % 4, t % 2
    g = {"x": gray(x), "y": gray(y), "z": gray(z)}
    mine = {a + "1": g[a] // 2 for a in g} | {a + "0": g[a] % 2 for a in g}
    other = {b: 1 - mine[b] for b in mine}

    def device(flips, core):
        at = {a: gray((other if a + "1" in flips else mine)[a + "1"] * 2 + (other if a + "0" in flips else mine)[a + "0"]) for a in g}
        return (at["z"] * 8 + at["y"] * 2 + core, at["x"])

    sent = []

    def send(src, dst, sem, to):
        copy = pltpu.make_async_remote_copy(src, dst, send_sem, sem, device_id=to, device_id_type=MESH)
        copy.start()
        sent.append(copy)

    def wait(ref, sem):
        pltpu.make_async_copy(ref, ref, sem).wait()

    load_amp = pltpu.make_async_copy(amp_hbm, amp, load_sem.at[0])
    load_amp.start()
    load_ints = [pltpu.make_async_copy(int_hbm.at[j], ints.at[j], load_sem.at[1 + j]) for j in range(4)]

    barrier = pltpu.get_barrier_semaphore()

    @pl.loop(1, 32)
    def _(k):
        to = ((z + k // 8) % 4) * 8 + ((y + (k // 2) % 4) % 4) * 2 + (c + k) % 2
        pl.semaphore_signal(barrier, inc=1, device_id=(to, x), device_id_type=MESH)

    for b in ("x0", "x1"):
        for core in range(2):
            pl.semaphore_signal(barrier, inc=1, device_id=device((b,), core), device_id_type=MESH)
    pl.semaphore_signal(barrier, inc=1, device_id=device(("x0", "x1"), c), device_id_type=MESH)
    for q in range(2):
        pl.semaphore_signal(barrier, inc=1, device_id=device(a_bits(q), c), device_id_type=MESH)

    def far(n):
        return ((2, x // 2), (2, 2 + x // 2), (1, 2 - x // 2), (3, 2 + x // 2))[n] + (x % 2,)

    load_amp.wait()
    for load in load_ints:
        load.start()
    away = lax.broadcasted_iota(I32, (32, 1024), 1) - 32 * lax.broadcasted_iota(I32, (32, 1024), 0)
    own_row = g["y"] * 2 + c
    near = [(dz, dy, dc) for dz, dy in ((1, 0), (1, 3), (3, 0), (3, 1), (0, 1), (0, 3), (0, 0), (0, 2)) for dc in (0, 1)]
    blocks = [far(n) for n in (2, 3, 0, 1)] + near
    for first in (0, 8, 16):
        some = blocks[first : first + 8]
        to = [((z + dz) % 4) * 8 + ((y + dy) % 4) * 2 + (c + dc) % 2 for dz, dy, dc in some]
        pick = [jnp.where(away == owner[p], 1.0, 0.0).astype(BF16) for p in to]
        pick = jnp.concatenate(pick, axis=0)
        for n in range(2):
            got = jnp.dot(pick, amp[:, n * 512 : n * 512 + 512], preferred_element_type=F32)
            ordered[first : first + len(some), :, n * 512 : n * 512 + 512] = got.astype(BF16).reshape(len(some), 32, 512)
        if first == 0:
            pl.semaphore_wait(barrier, 38)
        for i, p in enumerate(to):
            src, dst = ordered.at[first + i], column.at[g["z"], own_row]
            if some[i] == (0, 0, 0):
                pltpu.make_async_copy(src, dst, amp_sem.at[g["z"]]).start()
            elif first == 0 and i < 4:
                send(src, dst, far_sem.at[(2, 3, 0, 1)[i]], (p, x))
            else:
                send(src, dst, amp_sem.at[g["z"]], (p, x))

    for n in (2, 3, 0, 1):
        dz, dy, dc = far(n)
        gz = gray((z - dz + 4) % 4)
        block = column.at[gz, gray((y - dy + 4) % 4) * 2 + (c + dc) % 2]
        wait(block, far_sem.at[n])
        for dx in (1, 3, 2):
            send(block, block, amp_sem.at[gz], (t, (x + dx) % 4))

    for load in load_ints:
        load.wait()

    for k in CHUNKS:
        zv = {"z1": (other if k >> 1 else mine)["z1"], "z0": (other if k & 1 else mine)["z0"]}
        gz = zv["z1"] * 2 + zv["z0"]
        wait(column.at[gz, pl.ds(0, (8, 7, 7, 6)[k])], amp_sem.at[gz])

        @pl.loop(0, 4)
        def _(j):
            left_side = column[gz].reshape(256, 1024)
            got = jnp.dot(left_side, ints[j], preferred_element_type=F32).astype(BF16)
            gj = gray(j)
            pieces[gj // 2, gj % 2, zv["z1"], zv["z0"]] = got.reshape(2, 2, 2, 2, 16, 1024)

        flip_z = {"z0": k & 1, "z1": k >> 1}
        for q in range(2):
            xa, ya, za = a_bits(q)
            zb = "z" + str(1 - q)
            f = flip_z[za]
            sem = sem1.at[q, flip_z[zb]]

            def part(fx, fy, core):
                at = {xa: (other if fx else mine)[xa], ya: (other if fy else mine)[ya]} | zv
                return view(pieces, (), NAT, at, (core, q))

            def place(chip, a):
                return r1[q].at[chip, c, a, :, zv[zb], :]

            for core in range(2):
                send(part(1 - f, f, core), place(1, f), sem, device((xa,), core))
                send(part(f, 1 - f, core), place(2, f), sem, device((ya,), core))
                send(part(1 - f, 1 - f, core), place(3, 1 - f), sem, device((za,), core))
            send(part(f, f, 1 - c), place(0, f), sem, device((), 1 - c))
            pltpu.make_async_copy(part(f, f, c), place(0, f), sem).start()

    every = slice(None)

    def where(r, f1, f2, f3):
        b1, b2, b3 = b_bits(r)
        return {b: (other if f else mine)[b] for b, f in ((b1, f1), (b2, f2), (b3, f3))}

    def in_r1(r, at):
        q = STREAMS[r][0]
        return tuple(at[axis + str(1 - q)] for axis in "xzy")

    def in_r3(r, at):
        first = b_bits(r)[0]
        return tuple(at[b] for b in (axis + str(1 - STREAMS[r][0]) for axis in "xzy") if b != first)

    def columns(r):
        return pl.ds(STREAMS[r][1], STREAMS[r][2])

    def z_at(r):
        return [b[0] for b in b_bits(r)].index("z")

    halves = ((1, 1), (1, 0), (0, 1), (0, 0))

    def step3(r, a, f2, f3):
        at = where(r, 1, f2, f3)
        src = r1[STREAMS[r][0]].at[(every, every, a) + in_r1(r, at) + (every, columns(r))]
        dst = r3[r].at[(every, every, a) + in_r3(r, at)]
        send(src, dst, sem3.at[r, 4 * a + 2 * f2 + f3], device((b_bits(r)[0],), c))

    lane = lax.broadcasted_iota(I32, (8, 256), 1)
    bin_of_row = lax.broadcasted_iota(I32, (8, 256), 0)
    for n, (r, a, f) in enumerate(TABLES):
        q, b1 = STREAMS[r][0], b_bits(r)[0]
        xa, xb = "x" + str(q), "x" + str(1 - q)
        want = {xa: (other if a else mine)[xa], xb: (other if f else mine)[xb]}
        block = gray(want["x1"] * 2 + want["x0"])
        label = jnp.full((8, 256), -1, I32)
        for s in range(16):
            chip = (s >> 1) & 3
            tile, rep = device(([b1] if s >> 3 else []) + ([a_bits(q)[chip - 1]] if chip else []), s & 1)
            slot = rep * 4 + block
            found = jnp.where(live[slot, tile] != 0, screen[slot, tile] - 8 * block, -1)
            label = jnp.where(lane // 16 == s, found, label)
        hit = label == bin_of_row
        rows = [jnp.where(hit & (lane % 16 == m), 1.0, 0.0).astype(F32) for m in range(16)]
        weights[n] = jnp.concatenate(rows, axis=0).astype(BF16)

    for v in (1, 0):
        for q in range(2):
            zb = "z" + str(1 - q)
            wait(r1[q].at[:, :, :, :, (other if v else mine)[zb], :], sem1.at[q, v])
            for f2, f3 in halves:
                for r in range(3 * q, 3 * q + 3):
                    if (1, f2, f3)[z_at(r)] == v:
                        step3(r, 1, f2, f3)

    def step4(r, a, f2, f3):
        q = STREAMS[r][0]
        at = where(r, 0, f2, f3)
        wait(r3[r].at[(every, every, a) + in_r3(r, at)], sem3.at[r, 4 * a + 2 * f2 + f3])
        fx = {b_bits(r)[1]: f2, b_bits(r)[2]: f3}.get("x" + str(1 - q), 0)
        blocks = []
        for chip in range(4):
            for core in range(2):
                blocks.append(r1[q][(chip, core, a) + in_r1(r, at) + (every, columns(r))])
        for chip in range(4):
            for core in range(2):
                blocks.append(r3[r][(chip, core, a) + in_r3(r, at)])
        table = weights[TABLES.index((r, a, fx))]
        binned = jnp.dot(table, jnp.concatenate(blocks, axis=0), preferred_element_type=F32)
        if f2:
            s4[r][f3, a] = binned.astype(BF16)
            send(s4[r].at[f3, a], r4[r].at[f3, a], sem4.at[r, 2 * a + f3], device((b_bits(r)[1],), c))
        else:
            k4[r][f3, a] = binned

    def step5(r, a, f3):
        wait(r4[r].at[f3, a], sem4.at[r, 2 * a + f3])
        total = k4[r][f3, a] + r4[r][f3, a].astype(F32)
        if f3:
            s5[r][a] = total.astype(BF16)
            send(s5[r].at[a], r5[r].at[a], sem5.at[r, a], device((b_bits(r)[2],), c))
        else:
            k5[r][a] = total

    def home(r):
        wait(r5[r].at[1], sem5.at[r, 1])
        s6[r][...] = (k5[r][1] + r5[r][1].astype(F32)).astype(BF16)
        send(s6[r], r6[r], sem6.at[r], device(a_bits(STREAMS[r][0]), c))

    for n in range(1):
        for r in range(6):
            step3(r, 0, *halves[n])
    for a in (1, 0):
        for n, (f2, f3) in enumerate(halves):
            for r in range(6):
                step4(r, a, f2, f3)
                if a and n + 1 < 4:
                    step3(r, 0, *halves[n + 1])
            if f2 == 0:
                for r in range(6):
                    step5(r, a, f3)
            if (a, n) == (0, 1):
                for r in range(6):
                    home(r)
    for r, (q, start, width, _) in enumerate(STREAMS):
        wait(r5[r].at[0], sem5.at[r, 0])
        wait(r6[r], sem6.at[r])
        total = k5[r][0] + r5[r][0].astype(F32) + r6[r][...].astype(F32)
        out[16 * q : 16 * q + 16, :, start : start + width] = total.reshape(16, 8, width)

    for copy in sent:
        copy.wait_send()


def on_device(amplitudes, integrals, owner_order, screen_list, live_mask):
    rows, tiles, width = amplitudes.shape
    widths = [w for _, _, w, _ in STREAMS]

    def group(lead, tail, dtype):
        return [pltpu.VMEM(lead + tail(w), dtype) for w in widths]

    two = (2,)
    raw = lambda w: (16, w)
    dense = lambda w: (128, w)
    scratch = [
        pltpu.VMEM((rows * tiles, width), BF16),
        pltpu.VMEM((4, width, width), BF16),
        pltpu.VMEM((20, rows, width), BF16),
        pltpu.VMEM((4, 8, rows, width), BF16),
        pltpu.VMEM(two * 8 + (16, width), BF16),
        pltpu.VMEM((len(TABLES), 128, 256), BF16),
        *[pltpu.VMEM((4, 2, 2, 2, 2, 2, 16, width), BF16)] * 2,
        *group((4, 2, 2, 2, 2), raw, BF16),
        *group(two * 2, dense, BF16),
        *group(two * 2, dense, BF16),
        *group(two * 2, dense, F32),
        *group(two, dense, BF16),
        *group(two, dense, BF16),
        *group(two, dense, F32),
        *group((), dense, BF16),
        *group((), dense, BF16),
        pltpu.SemaphoreType.DMA((5,)),
        pltpu.SemaphoreType.DMA((4,)),
        pltpu.SemaphoreType.DMA((4,)),
        pltpu.SemaphoreType.DMA,
        pltpu.SemaphoreType.DMA((2, 2)),
        pltpu.SemaphoreType.DMA((6, 8)),
        pltpu.SemaphoreType.DMA((6, 4)),
        pltpu.SemaphoreType.DMA((6, 2)),
        pltpu.SemaphoreType.DMA((6,)),
    ]
    smem = pl.BlockSpec(memory_space=pltpu.SMEM)
    hbm = pl.BlockSpec(memory_space=pl.ANY)
    return pl.pallas_call(
        kernel,
        out_shape=jax.ShapeDtypeStruct((rows, 8, width), F32),
        in_specs=[smem, smem, smem, hbm, hbm],
        out_specs=pl.BlockSpec(memory_space=pltpu.VMEM),
        scratch_shapes=scratch,
        cost_estimate=pl.CostEstimate(flops=13_000_000_000, bytes_accessed=12 << 20, transcendentals=0),
        compiler_params=pltpu.CompilerParams(
            collective_id=0, has_side_effects=True, vmem_limit_bytes=60 << 20
        ),
    )(owner_order, screen_list.T, live_mask.T, amplitudes.reshape(rows * tiles, width), integrals[0])


def solution(mesh):
    in_specs = (P("tile", None, None), P("tile", "rep", None, None), P(), P(), P())
    out_specs = P("tile", "rep", None)
    return jax.shard_map(
        on_device, mesh=mesh, in_specs=in_specs, out_specs=out_specs, check_vma=False
    )
```

```python
import jax
import jax.numpy as jnp
from jax import lax
from jax.experimental import pallas as pl
from jax.experimental.pallas import tpu as pltpu
from jax.sharding import PartitionSpec as P

MESH = pl.DeviceIdType.MESH
BF16, F32, I32 = jnp.bfloat16, jnp.float32, jnp.int32
NAT = ("x1", "x0", "z1", "z0", "y1", "y0")
ORDER = ("x0", "y0", "z0", "x1", "y1", "z1")
STREAMS = ((0, 0, 384, 0), (0, 384, 384, 1), (0, 768, 256, 2), (1, 0, 384, 0), (1, 384, 384, 1), (1, 768, 256, 2))
CHUNKS = (1, 2, 3, 0)


def a_bits(q):
    return [axis + str(q) for axis in "xyz"]


def b_bits(r):
    q, first = STREAMS[r][0], STREAMS[r][3]
    return ["xyz"[(first + i) % 3] + str(1 - q) for i in range(3)]


def tables(r):
    ahead = b_bits(r)[0][0] == "x"
    return [(r, a, f) for a in range(2) for f in range(1 if ahead else 2)]


TABLES = [key for r in range(6) for key in tables(r)]


def gray(v):
    return v + v // 2 - 2 * (v // 3)


def view(ref, lead, names, fixed, tail=()):
    return ref.at[tuple(lead) + tuple(fixed[b] if b in fixed else slice(None) for b in names) + tuple(tail)]


def kernel(owner, screen, live, amp_hbm, int_hbm, out, amp, ints, ordered, column, pieces, weights, *rest):
    r1 = rest[:2]
    r3, s4, r4, k4, s5, r5, k5, s6, r6 = (rest[2 + 6 * i : 8 + 6 * i] for i in range(9))
    load_sem, amp_sem, far_sem, send_sem, sem1, sem3, sem4, sem5, sem6 = rest[56:]
    x, t = lax.axis_index("rep"), lax.axis_index("tile")
    z, y, c = t // 8, (t // 2) % 4, t % 2
    g = {"x": gray(x), "y": gray(y), "z": gray(z)}
    mine = {a + "1": g[a] // 2 for a in g} | {a + "0": g[a] % 2 for a in g}
    other = {b: 1 - mine[b] for b in mine}

    def device(flips, core):
        at = {a: gray((other if a + "1" in flips else mine)[a + "1"] * 2 + (other if a + "0" in flips else mine)[a + "0"]) for a in g}
        return (at["z"] * 8 + at["y"] * 2 + core, at["x"])

    sent = []

    def send(src, dst, sem, to):
        copy = pltpu.make_async_remote_copy(src, dst, send_sem, sem, device_id=to, device_id_type=MESH)
        copy.start()
        sent.append(copy)

    def wait(ref, sem):
        pltpu.make_async_copy(ref, ref, sem).wait()

    load_amp = pltpu.make_async_copy(amp_hbm, amp, load_sem.at[0])
    load_amp.start()
    load_ints = [pltpu.make_async_copy(int_hbm.at[j], ints.at[j], load_sem.at[1 + j]) for j in range(4)]

    barrier = pltpu.get_barrier_semaphore()

    @pl.loop(1, 32)
    def _(k):
        to = ((z + k // 8) % 4) * 8 + ((y + (k // 2) % 4) % 4) * 2 + (c + k) % 2
        pl.semaphore_signal(barrier, inc=1, device_id=(to, x), device_id_type=MESH)

    for b in ("x0", "x1"):
        for core in range(2):
            pl.semaphore_signal(barrier, inc=1, device_id=device((b,), core), device_id_type=MESH)
    pl.semaphore_signal(barrier, inc=1, device_id=device(("x0", "x1"), c), device_id_type=MESH)
    for q in range(2):
        pl.semaphore_signal(barrier, inc=1, device_id=device(a_bits(q), c), device_id_type=MESH)

    def far(n):
        return ((2, x // 2), (2, 2 + x // 2), (1, 2 - x // 2), (3, 2 + x // 2))[n] + (x % 2,)

    load_amp.wait()
    for load in load_ints:
        load.start()
    away = lax.broadcasted_iota(I32, (32, 1024), 1) - 32 * lax.broadcasted_iota(I32, (32, 1024), 0)
    own_row = g["y"] * 2 + c
    near = [(dz, dy, dc) for dz, dy in ((1, 0), (1, 3), (3, 0), (3, 1), (0, 1), (0, 3), (0, 0), (0, 2)) for dc in (0, 1)]
    blocks = [far(n) for n in (2, 3, 0, 1)] + near
    for first in (0, 8, 16):
        some = blocks[first : first + 8]
        to = [((z + dz) % 4) * 8 + ((y + dy) % 4) * 2 + (c + dc) % 2 for dz, dy, dc in some]
        pick = [jnp.where(away == owner[p], 1.0, 0.0).astype(BF16) for p in to]
        pick = jnp.concatenate(pick, axis=0)
        for n in range(2):
            got = jnp.dot(pick, amp[:, n * 512 : n * 512 + 512], preferred_element_type=F32)
            ordered[first : first + len(some), :, n * 512 : n * 512 + 512] = got.astype(BF16).reshape(len(some), 32, 512)
        if first == 0:
            pl.semaphore_wait(barrier, 38)
        for i, p in enumerate(to):
            src, dst = ordered.at[first + i], column.at[g["z"], own_row]
            if some[i] == (0, 0, 0):
                pltpu.make_async_copy(src, dst, amp_sem.at[g["z"]]).start()
            elif first == 0 and i < 4:
                send(src, dst, far_sem.at[(2, 3, 0, 1)[i]], (p, x))
            else:
                send(src, dst, amp_sem.at[g["z"]], (p, x))

    lane = lax.broadcasted_iota(I32, (8, 256), 1)
    bin_of_row = lax.broadcasted_iota(I32, (8, 256), 0)
    for n, (r, a, f) in enumerate(TABLES):
        q, b1 = STREAMS[r][0], b_bits(r)[0]
        xa, xb = "x" + str(q), "x" + str(1 - q)
        want = {xa: (other if a else mine)[xa], xb: (other if f else mine)[xb]}
        block = gray(want["x1"] * 2 + want["x0"])
        label = jnp.full((8, 256), -1, I32)
        for s in range(16):
            chip = (s >> 1) & 3
            tile, rep = device(([b1] if s >> 3 else []) + ([a_bits(q)[chip - 1]] if chip else []), s & 1)
            slot = rep * 4 + block
            found = jnp.where(live[slot, tile] != 0, screen[slot, tile] - 8 * block, -1)
            label = jnp.where(lane // 16 == s, found, label)
        hit = label == bin_of_row
        rows = [jnp.where(hit & (lane % 16 == m), 1.0, 0.0).astype(F32) for m in range(16)]
        weights[n] = jnp.concatenate(rows, axis=0).astype(BF16)

    for n in (2, 3, 0, 1):
        dz, dy, dc = far(n)
        gz = gray((z - dz + 4) % 4)
        block = column.at[gz, gray((y - dy + 4) % 4) * 2 + (c + dc) % 2]
        wait(block, far_sem.at[n])
        for dx in (1, 3, 2):
            send(block, block, amp_sem.at[gz], (t, (x + dx) % 4))

    for load in load_ints:
        load.wait()

    for k in CHUNKS:
        zv = {"z1": (other if k >> 1 else mine)["z1"], "z0": (other if k & 1 else mine)["z0"]}
        gz = zv["z1"] * 2 + zv["z0"]
        wait(column.at[gz, pl.ds(0, (8, 7, 7, 6)[k])], amp_sem.at[gz])

        @pl.loop(0, 4)
        def _(j):
            left_side = column[gz].reshape(256, 1024)
            got = jnp.dot(left_side, ints[j], preferred_element_type=F32).astype(BF16)
            gj = gray(j)
            pieces[gj // 2, gj % 2, zv["z1"], zv["z0"]] = got.reshape(2, 2, 2, 2, 16, 1024)

        flip_z = {"z0": k & 1, "z1": k >> 1}
        for q in range(2):
            xa, ya, za = a_bits(q)
            zb = "z" + str(1 - q)
            f = flip_z[za]
            sem = sem1.at[q, flip_z[zb]]

            def part(fx, fy, core):
                at = {xa: (other if fx else mine)[xa], ya: (other if fy else mine)[ya]} | zv
                return view(pieces, (), NAT, at, (core, q))

            def place(chip, a):
                return r1[q].at[chip, c, a, :, zv[zb], :]

            for core in range(2):
                send(part(1 - f, f, core), place(1, f), sem, device((xa,), core))
                send(part(f, 1 - f, core), place(2, f), sem, device((ya,), core))
                send(part(1 - f, 1 - f, core), place(3, 1 - f), sem, device((za,), core))
            send(part(f, f, 1 - c), place(0, f), sem, device((), 1 - c))
            pltpu.make_async_copy(part(f, f, c), place(0, f), sem).start()

    every = slice(None)

    def where(r, f1, f2, f3):
        b1, b2, b3 = b_bits(r)
        return {b: (other if f else mine)[b] for b, f in ((b1, f1), (b2, f2), (b3, f3))}

    def in_r1(r, at):
        q = STREAMS[r][0]
        return tuple(at[axis + str(1 - q)] for axis in "xzy")

    def in_r3(r, at):
        first = b_bits(r)[0]
        return tuple(at[b] for b in (axis + str(1 - STREAMS[r][0]) for axis in "xzy") if b != first)

    def columns(r):
        return pl.ds(STREAMS[r][1], STREAMS[r][2])

    def z_at(r):
        return [b[0] for b in b_bits(r)].index("z")

    halves = ((1, 1), (1, 0), (0, 1), (0, 0))

    def step3(r, a, f2, f3):
        at = where(r, 1, f2, f3)
        src = r1[STREAMS[r][0]].at[(every, every, a) + in_r1(r, at) + (every, columns(r))]
        dst = r3[r].at[(every, every, a) + in_r3(r, at)]
        send(src, dst, sem3.at[r, 4 * a + 2 * f2 + f3], device((b_bits(r)[0],), c))

    for v in (1, 0):
        for q in range(2):
            zb = "z" + str(1 - q)
            wait(r1[q].at[:, :, :, :, (other if v else mine)[zb], :], sem1.at[q, v])
            for f2, f3 in halves:
                for r in range(3 * q, 3 * q + 3):
                    if (1, f2, f3)[z_at(r)] == v:
                        step3(r, 1, f2, f3)

    def step4(r, a, f2, f3):
        q = STREAMS[r][0]
        at = where(r, 0, f2, f3)
        wait(r3[r].at[(every, every, a) + in_r3(r, at)], sem3.at[r, 4 * a + 2 * f2 + f3])
        fx = {b_bits(r)[1]: f2, b_bits(r)[2]: f3}.get("x" + str(1 - q), 0)
        blocks = []
        for chip in range(4):
            for core in range(2):
                blocks.append(r1[q][(chip, core, a) + in_r1(r, at) + (every, columns(r))])
        for chip in range(4):
            for core in range(2):
                blocks.append(r3[r][(chip, core, a) + in_r3(r, at)])
        table = weights[TABLES.index((r, a, fx))]
        binned = jnp.dot(table, jnp.concatenate(blocks, axis=0), preferred_element_type=F32)
        if f2:
            s4[r][f3, a] = binned.astype(BF16)
            send(s4[r].at[f3, a], r4[r].at[f3, a], sem4.at[r, 2 * a + f3], device((b_bits(r)[1],), c))
        else:
            k4[r][f3, a] = binned

    def step5(r, a, f3):
        wait(r4[r].at[f3, a], sem4.at[r, 2 * a + f3])
        total = k4[r][f3, a] + r4[r][f3, a].astype(F32)
        if f3:
            s5[r][a] = total.astype(BF16)
            send(s5[r].at[a], r5[r].at[a], sem5.at[r, a], device((b_bits(r)[2],), c))
        else:
            k5[r][a] = total

    def home(r):
        wait(r5[r].at[1], sem5.at[r, 1])
        s6[r][...] = (k5[r][1] + r5[r][1].astype(F32)).astype(BF16)
        send(s6[r], r6[r], sem6.at[r], device(a_bits(STREAMS[r][0]), c))

    for n in range(0):
        for r in range(6):
            step3(r, 0, *halves[n])
    for a in (1, 0):
        for n, (f2, f3) in enumerate(halves):
            for r in range(6):
                step4(r, a, f2, f3)
            if f2 == 0:
                for r in range(6):
                    step5(r, a, f3)
            if a and n + 0 < 4:
                for r in range(6):
                    step3(r, 0, *halves[n + 0])
            if (a, n) == (0, 1):
                for r in range(6):
                    home(r)
    for r, (q, start, width, _) in enumerate(STREAMS):
        wait(r5[r].at[0], sem5.at[r, 0])
        wait(r6[r], sem6.at[r])
        total = k5[r][0] + r5[r][0].astype(F32) + r6[r][...].astype(F32)
        out[16 * q : 16 * q + 16, :, start : start + width] = total.reshape(16, 8, width)

    for copy in sent:
        copy.wait_send()


def on_device(amplitudes, integrals, owner_order, screen_list, live_mask):
    rows, tiles, width = amplitudes.shape
    widths = [w for _, _, w, _ in STREAMS]

    def group(lead, tail, dtype):
        return [pltpu.VMEM(lead + tail(w), dtype) for w in widths]

    two = (2,)
    raw = lambda w: (16, w)
    dense = lambda w: (128, w)
    scratch = [
        pltpu.VMEM((rows * tiles, width), BF16),
        pltpu.VMEM((4, width, width), BF16),
        pltpu.VMEM((20, rows, width), BF16),
        pltpu.VMEM((4, 8, rows, width), BF16),
        pltpu.VMEM(two * 8 + (16, width), BF16),
        pltpu.VMEM((len(TABLES), 128, 256), BF16),
        *[pltpu.VMEM((4, 2, 2, 2, 2, 2, 16, width), BF16)] * 2,
        *group((4, 2, 2, 2, 2), raw, BF16),
        *group(two * 2, dense, BF16),
        *group(two * 2, dense, BF16),
        *group(two * 2, dense, F32),
        *group(two, dense, BF16),
        *group(two, dense, BF16),
        *group(two, dense, F32),
        *group((), dense, BF16),
        *group((), dense, BF16),
        pltpu.SemaphoreType.DMA((5,)),
        pltpu.SemaphoreType.DMA((4,)),
        pltpu.SemaphoreType.DMA((4,)),
        pltpu.SemaphoreType.DMA,
        pltpu.SemaphoreType.DMA((2, 2)),
        pltpu.SemaphoreType.DMA((6, 8)),
        pltpu.SemaphoreType.DMA((6, 4)),
        pltpu.SemaphoreType.DMA((6, 2)),
        pltpu.SemaphoreType.DMA((6,)),
    ]
    smem = pl.BlockSpec(memory_space=pltpu.SMEM)
    hbm = pl.BlockSpec(memory_space=pl.ANY)
    return pl.pallas_call(
        kernel,
        out_shape=jax.ShapeDtypeStruct((rows, 8, width), F32),
        in_specs=[smem, smem, smem, hbm, hbm],
        out_specs=pl.BlockSpec(memory_space=pltpu.VMEM),
        scratch_shapes=scratch,
        cost_estimate=pl.CostEstimate(flops=13_000_000_000, bytes_accessed=12 << 20, transcendentals=0),
        compiler_params=pltpu.CompilerParams(
            collective_id=0, has_side_effects=True, vmem_limit_bytes=60 << 20
        ),
    )(owner_order, screen_list.T, live_mask.T, amplitudes.reshape(rows * tiles, width), integrals[0])


def solution(mesh):
    in_specs = (P("tile", None, None), P("tile", "rep", None, None), P(), P(), P())
    out_specs = P("tile", "rep", None)
    return jax.shard_map(
        on_device, mesh=mesh, in_specs=in_specs, out_specs=out_specs, check_vma=False
    )
```
